256 devices in a mesh: rowblk: 16 (over z, x_lo), colblk: 16 (over x_hi, y, core).
Axes of the slice: x: 4 (x_hi: 2, x_lo: 2; x = x_hi * 2 + x_lo), y: 4, z: 8, core: 2. Of those that a mesh axis runs over, the one named last changes fastest.
Arguments:
- points: bfloat16 [65536, 128], P(('rowblk', 'colblk')), may hold values from -6 to 6
- spread: float32 [1], replicated, may hold values from 2.5 to 3.5
- panel: bfloat16 [65536, 32], P(('rowblk', 'colblk')), may hold values from -6 to 6
Outputs:
- refined: float32 [32, 65536], P(None, ('rowblk', 'colblk'))
The draws below stay inside these ranges and needn't reach their ends.
All inputs are finite; a program needn't handle non-finite values.
Results may differ from the reference program's by a relative error of at most 0.0055.
Values may be sent and summed in bfloat16 or wider, within the bound.
A program may use at most 64 MiB of HBM per device.

```python
import math
import jax
import jax.numpy as jnp
from jax import lax

WIDTH = 128
KCOL = 32
NPTS = 65536


def block_levels(key, shape, pieces, smallest, high):
    def one(position, blocks):
        heights = jax.random.uniform(jax.random.fold_in(jax.random.fold_in(key, 6), position), (blocks,), jnp.float32, smallest / len(pieces), high / len(pieces))
        return jnp.repeat(jnp.exp(heights), shape[position] // blocks).reshape((-1,) + (1,) * (len(shape) - position - 1))

    gain = one(*pieces[0])
    for cut in pieces[1:]:
        gain = gain * one(*cut)
    return gain


def centred(rng, dims, deviation, most, split=(), kind=jnp.bfloat16):
    entries = jax.random.normal(rng, dims, jnp.float32) * deviation
    if len(split) > 0:
        entries = block_levels(rng, dims, split, -0.22, 0.18) * entries
    return jnp.clip(entries, min=-most, max=most).astype(kind)


def setup_inputs(seed: int = 0) -> dict:
    key_of = jax.random.split(jax.random.key(seed), 4)
    return {
        "points": centred(key_of[0], (NPTS, WIDTH), 1.0, 6.0, ((0, 256),)),
        "spread": jnp.clip(jnp.exp(jax.random.uniform(key_of[1], (1,), jnp.float32, math.log(2.5), math.log(3.5))), 2.5, 3.5),
        "panel": centred(key_of[2], (NPTS, KCOL), 1.0, 6.0, ((0, 256),)),
    }


def reference(points, spread, panel):
    pts = points.astype(jnp.float32)
    values = panel.astype(jnp.float32)
    sq = lax.optimization_barrier(jnp.sum(pts * pts, axis=1))
    coef = -0.5 / (spread[0] * spread[0])
    block = math.gcd(NPTS, 1024)
    all_ids = jnp.arange(NPTS, dtype=jnp.int32)

    def one_block(start):
        rows = lax.dynamic_slice_in_dim(pts, start, block, 0)
        rows_sq = lax.dynamic_slice_in_dim(sq, start, block, 0)
        inner = jnp.dot(rows, pts.T, precision=lax.Precision.HIGHEST, preferred_element_type=jnp.float32)
        expo = (rows_sq[:, None] + sq[None, :] - 2.0 * inner) * coef
        row_ids = start + jnp.arange(block, dtype=jnp.int32)
        affinity = jnp.where(row_ids[:, None] != all_ids[None, :], jnp.exp(expo), jnp.float32(0.0))
        affinity = affinity.astype(jnp.bfloat16).astype(jnp.float32)
        degree = lax.optimization_barrier(jnp.sum(affinity, axis=1))
        product = jnp.dot(affinity, values, precision=lax.Precision.HIGHEST, preferred_element_type=jnp.float32)
        return product / degree[:, None]
    starts = (jnp.arange(NPTS // block, dtype=jnp.int32) * block).astype(jnp.int32)
    walked = lax.map(one_block, starts).reshape(NPTS, KCOL)
    scale = jnp.sqrt(lax.optimization_barrier(jnp.mean(walked * walked, axis=0)) + 1e-06)
    return (walked / scale[None, :]).T
```

```python
import functools
import math

import jax
import jax.numpy as jnp
from jax import lax
from jax.experimental import pallas as pl
from jax.experimental.pallas import tpu as pltpu

MESH = pl.DeviceIdType.MESH
LOG2E = math.log2(math.e)
B = 256
W = 128
KC = 32
KR = 48
AUG = 16
NX, NY, NZ = 4, 4, 8


def three_terms(v):
    hi = v.astype(jnp.bfloat16)
    rest = v - hi.astype(jnp.float32)
    mid = rest.astype(jnp.bfloat16)
    lo = (rest - mid.astype(jnp.float32)).astype(jnp.bfloat16)
    return hi, mid, lo


def kernel(
    total,
    spread_ref, points_ref, panel_ref, out_ref,
    rows, cols, colaug, pt, acc, sendp, recvp, st_send, st_recv,
    row_s, row_r, col_s, col_r, colp_s, colp_r, red_s, red_r, a_s, a_r, b_s, b_r,
):
    r = lax.axis_index("rowblk")
    c = lax.axis_index("colblk")
    z, xl = r // 2, r % 2
    xh, y, core = c // 8, (c // 2) % 4, c % 2
    x = xh * 2 + xl

    def dev(xx, yy, zz, cc):
        return {"rowblk": zz * 2 + xx % 2, "colblk": ((xx // 2) * 4 + yy) * 2 + cc}

    def plane(s):
        dx, dy = s // 4, s % 4
        return dev((x + dx) % 4, (y + dy) % 4, z, core)

    def plane_back(s):
        dx, dy = s // 4, s % 4
        return ((4 - dx) % 4) * 4 + (4 - dy) % 4

    def line(s):
        dz, dc = s // 2, s % 2
        return dev(x, y, (z + dz) % 8, (core + dc) % 2)

    def line_back(s):
        dz, dc = s // 2, s % 2
        return ((8 - dz) % 8) * 2 + dc

    barrier = pltpu.get_barrier_semaphore()
    for s in range(1, 16):
        pl.semaphore_signal(barrier, inc=1, device_id=plane(s), device_id_type=MESH)
        pl.semaphore_signal(barrier, inc=1, device_id=line(s), device_id_type=MESH)

    pts = points_ref[...]
    ptsf = pts.astype(jnp.float32)
    ptst = ptsf.T
    sq = -0.5 * jnp.sum(ptst * ptst, axis=0, keepdims=True)
    hi, mid, lo = three_terms(sq)
    row = lax.broadcasted_iota(jnp.int32, (AUG, B), 0)
    f = lambda t: t.astype(jnp.float32)
    aug = jnp.where(row == 0, f(hi), jnp.where(row == 1, f(mid), jnp.where(row == 2, f(lo), 0.0)))
    aug = jnp.where((row >= 3) & (row < 6), 1.0, aug)
    rows[0, :W, :] = ptst.astype(jnp.bfloat16)
    rows[0, W:W + AUG, :] = aug.astype(jnp.bfloat16)
    cols[0] = pts
    pt[0, :KC, :] = panel_ref[...]

    pl.semaphore_wait(barrier, 30)

    row_copies, col_copies = [], []
    for s in range(1, 16):
        cp = pltpu.make_async_remote_copy(
            src_ref=rows.at[0, pl.ds(0, W + AUG)], dst_ref=rows.at[plane_back(s), pl.ds(0, W + AUG)],
            send_sem=row_s.at[s], recv_sem=row_r.at[plane_back(s)],
            device_id=plane(s), device_id_type=MESH)
        cp.start()
        row_copies.append(cp)
        cp = pltpu.make_async_remote_copy(
            src_ref=cols.at[0], dst_ref=cols.at[line_back(s)],
            send_sem=col_s.at[s], recv_sem=col_r.at[line_back(s)],
            device_id=line(s), device_id_type=MESH)
        cp.start()
        cp2 = pltpu.make_async_remote_copy(
            src_ref=pt.at[0, pl.ds(0, KC)], dst_ref=pt.at[line_back(s), pl.ds(0, KC)],
            send_sem=colp_s.at[s], recv_sem=colp_r.at[line_back(s)],
            device_id=line(s), device_id_type=MESH)
        cp2.start()
        col_copies.append((cp, cp2))

    tail = jnp.where(lax.broadcasted_iota(jnp.int32, (KR - KC, B), 0) == 0, 1.0, 0.0).astype(jnp.bfloat16)

    def fill(s, _):
        rows[s, W + AUG:, :] = jnp.zeros((W - AUG, B), jnp.bfloat16)
        pt[s, KC:, :] = tail
        return 0
    lax.fori_loop(0, 16, fill, 0)
    acc[...] = jnp.zeros_like(acc)

    coef = LOG2E / (spread_ref[0] * spread_ref[0])

    def column_block(s, masked):
        xj = cols[s]
        xf = xj.astype(jnp.float32)
        sqj = -0.5 * jnp.sum(xf * xf, axis=1, keepdims=True)
        jh, jm, jl = three_terms(sqj)
        lane = lax.broadcasted_iota(jnp.int32, (B, W), 1)
        ja = jnp.where(lane < 3, 1.0, jnp.where(lane == 3, f(jh), jnp.where(lane == 4, f(jm), jnp.where(lane == 5, f(jl), 0.0))))
        lhs = jnp.concatenate([xj, ja.astype(jnp.bfloat16)], axis=1)
        for i in range(16):
            g = jnp.dot(lhs, rows[i], preferred_element_type=jnp.float32)
            a = jnp.exp2(g * coef)
            if masked and i == 0:
                eye = lax.broadcasted_iota(jnp.int32, (B, B), 0) == lax.broadcasted_iota(jnp.int32, (B, B), 1)
                a = jnp.where(eye, 0.0, a)
            acc[i] += jnp.dot(pt[s], a.astype(jnp.bfloat16), preferred_element_type=jnp.float32)

    for cp in row_copies:
        cp.wait_recv()
    column_block(0, True)

    def step(s, _):
        pltpu.make_async_remote_copy(
            src_ref=cols.at[0], dst_ref=cols.at[s], send_sem=col_s.at[s], recv_sem=col_r.at[s],
            device_id=line(1), device_id_type=MESH).wait_recv()
        pltpu.make_async_remote_copy(
            src_ref=pt.at[0, pl.ds(0, KC)], dst_ref=pt.at[s, pl.ds(0, KC)], send_sem=colp_s.at[s], recv_sem=colp_r.at[s],
            device_id=line(1), device_id_type=MESH).wait_recv()
        column_block(s, False)
        return 0
    lax.fori_loop(1, 16, step, 0)

    red = []
    for s in range(1, 16):
        cp = pltpu.make_async_remote_copy(
            src_ref=acc.at[s, pl.ds(0, 40)], dst_ref=recvp.at[plane_back(s)],
            send_sem=red_s.at[s], recv_sem=red_r.at[plane_back(s)],
            device_id=plane(s), device_id_type=MESH)
        cp.start()
        red.append(cp)
    sums = acc[0, :40, :]
    for cp in red:
        cp.wait_recv()
    for s in range(1, 16):
        sums = sums + recvp[s]
    walked = sums[:KC, :] / sums[KC:KC + 1, :]

    part = jnp.sum(walked * walked, axis=1, keepdims=True)
    diag = lax.broadcasted_iota(jnp.int32, (KC, 128), 0) == lax.broadcasted_iota(jnp.int32, (KC, 128), 1)
    flat = jnp.sum(jnp.where(diag, part, 0.0), axis=0, keepdims=True)

    def stage(k, flat, where, back, ss, rs):
        st_send[k] = jnp.broadcast_to(flat, (8, 128))
        cps = []
        for s in range(1, 16):
            cp = pltpu.make_async_remote_copy(
                src_ref=st_send.at[k], dst_ref=st_recv.at[k, back(s)],
                send_sem=ss.at[s], recv_sem=rs.at[back(s)],
                device_id=where(s), device_id_type=MESH)
            cp.start()
            cps.append(cp)
        for cp in cps:
            cp.wait_recv()
        for s in range(1, 16):
            flat = flat + st_recv[k, s, 0:1, :]
        return flat, cps

    flat, c1 = stage(0, flat, plane, plane_back, a_s, a_r)
    flat, c2 = stage(1, flat, line, line_back, b_s, b_r)
    mean = jnp.sum(jnp.where(diag, jnp.broadcast_to(flat, (KC, 128)), 0.0), axis=1, keepdims=True) / total
    out_ref[...] = walked / jnp.sqrt(mean + 1e-6)

    for cp in row_copies + red + c1 + c2:
        cp.wait_send()
    for cp, cp2 in col_copies:
        cp.wait_send()
        cp2.wait_send()


def per_device(total, points, spread, panel):
    dma = pltpu.SemaphoreType.DMA((16,))
    return pl.pallas_call(
        functools.partial(kernel, total),
        out_shape=jax.ShapeDtypeStruct((KC, B), jnp.float32),
        in_specs=[pl.BlockSpec(memory_space=pltpu.SMEM)] + [pl.BlockSpec(memory_space=pltpu.VMEM)] * 2,
        out_specs=pl.BlockSpec(memory_space=pltpu.VMEM),
        scratch_shapes=[
            pltpu.VMEM((16, 2 * W, B), jnp.bfloat16),
            pltpu.VMEM((16, B, W), jnp.bfloat16),
            pltpu.VMEM((16, B, W), jnp.bfloat16),
            pltpu.VMEM((16, KR, B), jnp.bfloat16),
            pltpu.VMEM((16, KR, B), jnp.float32),
            pltpu.VMEM((16, 40, B), jnp.float32),
            pltpu.VMEM((16, 40, B), jnp.float32),
            pltpu.VMEM((2, 8, 128), jnp.float32),
            pltpu.VMEM((2, 16, 8, 128), jnp.float32),
        ] + [dma] * 12,
        compiler_params=pltpu.CompilerParams(
            collective_id=0, has_side_effects=True, vmem_limit_bytes=48 << 20),
        cost_estimate=pl.CostEstimate(flops=2 * 4096 * 4096 * 160, bytes_accessed=1 << 20, transcendentals=4096 * 4096),
        name="walk",
    )(spread, points, panel.T)


def solution(mesh):
    P = jax.sharding.PartitionSpec
    total = float(B * mesh.size)
    return jax.shard_map(
        functools.partial(per_device, total),
        mesh=mesh,
        in_specs=(P(("rowblk", "colblk"), None), P(), P(("rowblk", "colblk"), None)),
        out_specs=P(None, ("rowblk", "colblk")),
        check_vma=False,
    )
```

```python
import functools
import math

import jax
import jax.numpy as jnp
from jax import lax
from jax.experimental import pallas as pl
from jax.experimental.pallas import tpu as pltpu

MESH = pl.DeviceIdType.MESH
LOG2E = math.log2(math.e)
B = 256
W = 128
KC = 32
KR = 48
KS = 40
AUG = 16
G = 4
MSG = B + 2 * KC

PLANE = (
    (0, 0), (0, 1), (0, 3), (1, 0), (3, 0), (0, 2), (1, 1), (1, 3),
    (2, 0), (3, 1), (3, 3), (1, 2), (2, 1), (2, 3), (3, 2), (2, 2),
)
LINE = tuple((dz, dc) for dz in (0, 1, 7, 2, 6, 3, 5, 4) for dc in (0, 1))


def plane_back(s):
    dx, dy = PLANE[s]
    return PLANE.index(((4 - dx) % 4, (4 - dy) % 4))


def line_back(s):
    dz, dc = LINE[s]
    return LINE.index(((8 - dz) % 8, dc))


def three_terms(v):
    hi = v.astype(jnp.bfloat16).astype(jnp.float32)
    mid = (v - hi).astype(jnp.bfloat16).astype(jnp.float32)
    return hi, mid, v - hi - mid


def kernel(
    total,
    spread_ref, points_ref, panel_ref, out_ref,
    rows, cols, colaug, acc, recvp, st_send, st_recv,
    row_s, row_r, col_s, col_r, sib_s, fwd_s, red_s, red_r, a_s, a_r, b_s, b_r,
):
    r = lax.axis_index("rowblk")
    c = lax.axis_index("colblk")
    z, xl = r // 2, r % 2
    xh, y, core = c // 8, (c // 2) % 4, c % 2
    x = xh * 2 + xl

    def dev(xx, yy, zz, cc):
        return {"rowblk": zz * 2 + xx % 2, "colblk": ((xx // 2) * 4 + yy) * 2 + cc}

    def plane(s):
        dx, dy = PLANE[s]
        return dev((x + dx) % 4, (y + dy) % 4, z, core)

    def line(s):
        dz, dc = LINE[s]
        return dev(x, y, (z + dz) % 8, (core + dc) % 2)

    barrier = pltpu.get_barrier_semaphore()
    for s in range(1, 16):
        pl.semaphore_signal(barrier, inc=1, device_id=plane(s), device_id_type=MESH)
        pl.semaphore_signal(barrier, inc=1, device_id=line(s), device_id_type=MESH)

    pts = points_ref[...]
    ptst = pts.astype(jnp.float32).T
    hi, mid, lo = three_terms(-0.5 * jnp.sum(ptst * ptst, axis=0, keepdims=True))
    row = lax.broadcasted_iota(jnp.int32, (AUG, B), 0)
    aug = jnp.where(row == 0, hi, jnp.where(row == 1, mid, jnp.where(row == 2, lo, 0.0)))
    aug = jnp.where((row >= 3) & (row < 6), 1.0, aug)
    rows[0, :W, :] = ptst.astype(jnp.bfloat16)
    rows[0, W:W + AUG, :] = aug.astype(jnp.bfloat16)
    cols[0, :B, :] = pts
    cols[0, B:B + KC, :] = panel_ref[:, :W]
    cols[0, B + KC:, :] = panel_ref[:, W:]

    def fill(s, _):
        rows[s, W + AUG:, :] = jnp.zeros((W - AUG, B), jnp.bfloat16)
        return 0
    lax.fori_loop(0, 16, fill, 0)
    acc[...] = jnp.zeros_like(acc)

    coef = LOG2E / (spread_ref[0] * spread_ref[0])

    def augment(s):
        xf = cols[s, :B, :].astype(jnp.float32)
        jh, jm, jl = three_terms(-0.5 * jnp.sum(xf * xf, axis=1, keepdims=True))
        lane = lax.broadcasted_iota(jnp.int32, (B, W), 1)
        ja = jnp.where(lane == 3, jh, jnp.where(lane == 4, jm, jnp.where(lane == 5, jl, 0.0)))
        colaug[s] = jnp.where(lane < 3, 1.0, ja).astype(jnp.bfloat16)

    augment(0)

    pl.semaphore_wait(barrier, 30)

    def row_copy(s):
        t = plane_back(s)
        return pltpu.make_async_remote_copy(
            src_ref=rows.at[0, pl.ds(0, W + AUG)], dst_ref=rows.at[t, pl.ds(0, W + AUG)],
            send_sem=row_s.at[s], recv_sem=row_r.at[t], device_id=plane(s), device_id_type=MESH)

    def col_copy(src, dst, sem, where):
        return pltpu.make_async_remote_copy(
            src_ref=cols.at[src], dst_ref=cols.at[dst],
            send_sem=sem, recv_sem=col_r.at[dst], device_id=where, device_id_type=MESH)

    def sibling_copy(s):
        return col_copy(s, s + 1, sib_s.at[s // 2], line(1))

    def wait_col(s):
        col_copy(0, s, sib_s.at[0], line(1)).wait_recv()

    col_sends = [sibling_copy(0)]
    col_sends += [col_copy(0, line_back(s), col_s.at[s], line(s)) for s in (2, 4, 6, 8)]
    row_sends = [row_copy(s) for s in range(1, 16)]
    for cp in col_sends[:3] + row_sends[:3] + col_sends[3:] + row_sends[3:]:
        cp.start()

    pass_on = {
        6: col_copy(6, 10, fwd_s.at[0], line(4)),
        8: col_copy(8, 12, fwd_s.at[1], line(2)),
        10: col_copy(10, 14, fwd_s.at[2], line(4)),
    }
    siblings = {s: sibling_copy(s) for s in range(2, 16, 2)}

    wait_col(2)
    siblings[2].start()
    wait_col(1)
    augment(1)
    augment(2)
    wait_col(3)
    augment(3)

    def reduce_copy(s):
        t = plane_back(s)
        return pltpu.make_async_remote_copy(
            src_ref=acc.at[s, pl.ds(0, KS)], dst_ref=recvp.at[t],
            send_sem=red_s.at[s], recv_sem=red_r.at[t], device_id=plane(s), device_id_type=MESH)

    red = {s: reduce_copy(s) for s in range(1, 16)}
    ones = jnp.where(lax.broadcasted_iota(jnp.int32, (KR - KC, G * B), 0) == 0, 1.0, 0.0).astype(jnp.bfloat16)

    def step(t, _):
        cg = t // 4
        rg = jnp.where(t < 12, t % 4, 3 - t % 4)
        for k in range(0, 12, 2):
            @pl.when(t == k)
            def _():
                s = k + 4
                wait_col(s)
                if s in pass_on:
                    pass_on[s].start()
                siblings[s].start()

            @pl.when(t == k + 1)
            def _():
                wait_col(k + 5)

        for k in range(4):
            @pl.when(t == k)
            def _():
                for s in range(4 * k, 4 * k + 4):
                    if s:
                        row_copy(plane_back(s)).wait_recv()

        c0, r0 = cg * G, rg * G
        chunk = cols[pl.ds(c0, G)]
        lhs = jnp.concatenate(
            [chunk[:, :B].reshape(G * B, W), colaug[pl.ds(c0, G)].reshape(G * B, W)], axis=1)
        pt = jnp.concatenate(
            [chunk[k, B + h * KC:B + (h + 1) * KC] for k in range(G) for h in range(2)], axis=1)
        pt = jnp.concatenate([pt, ones], axis=0)
        rhs = jnp.concatenate([rows[r0 + k] for k in range(G)], axis=1)
        g = jnp.dot(lhs, rhs, preferred_element_type=jnp.float32)
        a = jnp.exp2(g * coef)
        eye = lax.broadcasted_iota(jnp.int32, (B, B), 0) == lax.broadcasted_iota(jnp.int32, (B, B), 1)
        first = jnp.where(eye & (t == 0), 0.0, a[:B, :B])
        a = jnp.concatenate([jnp.concatenate([first, a[:B, B:]], axis=1), a[B:]], axis=0)
        o = jnp.dot(pt, a.astype(jnp.bfloat16), preferred_element_type=jnp.float32)
        for k in range(G):
            acc[r0 + k] += o[:, k * B:(k + 1) * B]

        augment(jnp.minimum(t + 4, 15))

        for k in range(12, 15):
            @pl.when(t == k)
            def _():
                for s in range(4 * (15 - k), 4 * (15 - k) + 4):
                    red[s].start()
        return 0

    lax.fori_loop(0, 16, step, 0)
    for s in range(1, 4):
        red[s].start()
    sums = acc[0, :KS, :]
    for s in range(15, 0, -1):
        red[plane_back(s)].wait_recv()
        sums = sums + recvp[s]
    walked = sums[:KC, :] / sums[KC:KC + 1, :]

    part = jnp.sum(walked * walked, axis=1, keepdims=True)
    diag = lax.broadcasted_iota(jnp.int32, (KC, 128), 0) == lax.broadcasted_iota(jnp.int32, (KC, 128), 1)
    flat = jnp.sum(jnp.where(diag, part, 0.0), axis=0, keepdims=True)

    def stage(k, flat, where, back, ss, rs):
        st_send[k] = jnp.broadcast_to(flat, (8, 128))
        cps = []
        for s in range(15, 0, -1):
            cp = pltpu.make_async_remote_copy(
                src_ref=st_send.at[k], dst_ref=st_recv.at[k, back(s)],
                send_sem=ss.at[s], recv_sem=rs.at[back(s)],
                device_id=where(s), device_id_type=MESH)
            cp.start()
            cps.append(cp)
        for cp in cps:
            cp.wait_recv()
        for s in range(1, 16):
            flat = flat + st_recv[k, s, 0:1, :]
        return flat, cps

    flat, c1 = stage(0, flat, plane, plane_back, a_s, a_r)
    flat, c2 = stage(1, flat, line, line_back, b_s, b_r)
    mean = jnp.sum(jnp.where(diag, jnp.broadcast_to(flat, (KC, 128)), 0.0), axis=1, keepdims=True) / total
    out_ref[...] = walked / jnp.sqrt(mean + 1e-6)

    for cp in row_sends + col_sends + list(siblings.values()) + list(pass_on.values()) + list(red.values()) + c1 + c2:
        cp.wait_send()


def per_device(total, points, spread, panel):
    dma = pltpu.SemaphoreType.DMA((16,))
    return pl.pallas_call(
        functools.partial(kernel, total),
        out_shape=jax.ShapeDtypeStruct((KC, B), jnp.float32),
        in_specs=[pl.BlockSpec(memory_space=pltpu.SMEM)] + [pl.BlockSpec(memory_space=pltpu.VMEM)] * 2,
        out_specs=pl.BlockSpec(memory_space=pltpu.VMEM),
        scratch_shapes=[
            pltpu.VMEM((16, 2 * W, B), jnp.bfloat16),
            pltpu.VMEM((16, MSG, W), jnp.bfloat16),
            pltpu.VMEM((16, B, W), jnp.bfloat16),
            pltpu.VMEM((16, KR, B), jnp.float32),
            pltpu.VMEM((16, KS, B), jnp.float32),
            pltpu.VMEM((2, 8, 128), jnp.float32),
            pltpu.VMEM((2, 16, 8, 128), jnp.float32),
        ] + [dma] * 12,
        compiler_params=pltpu.CompilerParams(
            collective_id=0, has_side_effects=True, vmem_limit_bytes=48 << 20),
        cost_estimate=pl.CostEstimate(flops=2 * 4096 * 4096 * 160, bytes_accessed=1 << 20, transcendentals=4096 * 4096),
        name="walk",
    )(spread, points, panel.T)


def solution(mesh):
    P = jax.sharding.PartitionSpec
    total = float(B * mesh.size)
    return jax.shard_map(
        functools.partial(per_device, total),
        mesh=mesh,
        in_specs=(P(("rowblk", "colblk"), None), P(), P(("rowblk", "colblk"), None)),
        out_specs=P(None, ("rowblk", "colblk")),
        check_vma=False,
    )
```

```python
import functools
import math

import jax
import jax.numpy as jnp
from jax import lax
from jax.experimental import pallas as pl
from jax.experimental.pallas import tpu as pltpu

MESH = pl.DeviceIdType.MESH
LOG2E = math.log2(math.e)
B = 256
W = 128
KC = 32
KR = 48
KS = 40
AUG = 16
G = 4
HALF = 80
MSG = B + 2 * KC

PLANE = (
    (0, 0), (0, 1), (0, 3), (1, 0), (3, 0), (0, 2), (2, 0), (1, 1),
    (1, 3), (3, 1), (3, 3), (1, 2), (2, 1), (2, 3), (3, 2), (2, 2),
)
LINE = tuple((dz, dc) for dz in (0, 1, 7, 2, 6, 3, 5, 4) for dc in (0, 1))


def plane_back(s):
    dx, dy = PLANE[s]
    return PLANE.index(((4 - dx) % 4, (4 - dy) % 4))


def line_back(s):
    dz, dc = LINE[s]
    return LINE.index(((8 - dz) % 8, dc))


def three_terms(v):
    hi = v.astype(jnp.bfloat16).astype(jnp.float32)
    mid = (v - hi).astype(jnp.bfloat16).astype(jnp.float32)
    return hi, mid, v - hi - mid


def kernel(
    total,
    spread_ref, points_ref, panel_ref, out_ref,
    rows, cols, colaug, acc, recvp, st_send, st_recv,
    row_s, row_r, rowa_s, rowa_r, rowb_s, rowb_r, col_s, col_r, sib_s, fwd_s, red_s, red_r, a_s, a_r, b_s, b_r,
):
    r = lax.axis_index("rowblk")
    c = lax.axis_index("colblk")
    z, xl = r // 2, r % 2
    xh, y, core = c // 8, (c // 2) % 4, c % 2
    x = xh * 2 + xl

    def dev(xx, yy, zz, cc):
        return {"rowblk": zz * 2 + xx % 2, "colblk": ((xx // 2) * 4 + yy) * 2 + cc}

    def plane(s):
        dx, dy = PLANE[s]
        return dev((x + dx) % 4, (y + dy) % 4, z, core)

    def line(s):
        dz, dc = LINE[s]
        return dev(x, y, (z + dz) % 8, (core + dc) % 2)

    barrier = pltpu.get_barrier_semaphore()
    for s in range(1, 16):
        pl.semaphore_signal(barrier, inc=1, device_id=plane(s), device_id_type=MESH)
        pl.semaphore_signal(barrier, inc=1, device_id=line(s), device_id_type=MESH)

    pts = points_ref[...]
    ptst = pts.astype(jnp.float32).T
    hi, mid, lo = three_terms(-0.5 * jnp.sum(ptst * ptst, axis=0, keepdims=True))
    row = lax.broadcasted_iota(jnp.int32, (AUG, B), 0)
    aug = jnp.where(row == 0, hi, jnp.where(row == 1, mid, jnp.where(row == 2, lo, 0.0)))
    aug = jnp.where((row >= 3) & (row < 6), 1.0, aug)
    rows[0, :W, :] = ptst.astype(jnp.bfloat16)
    rows[0, W:W + AUG, :] = aug.astype(jnp.bfloat16)
    cols[0, :B, :] = pts
    cols[0, B:B + KC, :] = panel_ref[:, :W]
    cols[0, B + KC:, :] = panel_ref[:, W:]

    def fill(s, _):
        rows[s, W + AUG:, :] = jnp.zeros((W - AUG, B), jnp.bfloat16)
        return 0
    lax.fori_loop(0, 16, fill, 0)
    acc[...] = jnp.zeros_like(acc)

    coef = LOG2E / (spread_ref[0] * spread_ref[0])

    def augment(s):
        xf = cols[s, :B, :].astype(jnp.float32)
        jh, jm, jl = three_terms(-0.5 * jnp.sum(xf * xf, axis=1, keepdims=True))
        lane = lax.broadcasted_iota(jnp.int32, (B, W), 1)
        ja = jnp.where(lane == 3, jh, jnp.where(lane == 4, jm, jnp.where(lane == 5, jl, 0.0)))
        colaug[s] = jnp.where(lane < 3, 1.0, ja).astype(jnp.bfloat16)

    augment(0)

    pl.semaphore_wait(barrier, 30)

    def row_copy(s):
        t = plane_back(s)
        return pltpu.make_async_remote_copy(
            src_ref=rows.at[0, pl.ds(0, W + AUG)], dst_ref=rows.at[t, pl.ds(0, W + AUG)],
            send_sem=row_s.at[s], recv_sem=row_r.at[t], device_id=plane(s), device_id_type=MESH)

    def half_copy(src, to, dst, part, ss, rs):
        return pltpu.make_async_remote_copy(
            src_ref=rows.at[src, part], dst_ref=rows.at[dst, part],
            send_sem=ss.at[dst], recv_sem=rs.at[dst], device_id=plane(to), device_id_type=MESH)

    row_pass = {}
    for e in (1, 3, 2):
        for d in (1, 3, 2):
            src, to = PLANE.index((0, d)), PLANE.index((e, 0))
            row_pass.setdefault(src, []).append(
                half_copy(src, to, PLANE.index(((4 - e) % 4, d)), pl.ds(0, HALF), rowa_s, rowa_r))
            src, to = PLANE.index((d, 0)), PLANE.index((0, e))
            row_pass.setdefault(src, []).append(
                half_copy(src, to, PLANE.index((d, (4 - e) % 4)), pl.ds(HALF, W + AUG - HALF), rowb_s, rowb_r))

    def row_in(s):
        row_copy(plane_back(s)).wait_recv()
        for cp in row_pass[s]:
            cp.start()

    def halves_in(s):
        half_copy(0, 1, s, pl.ds(0, HALF), rowa_s, rowa_r).wait_recv()
        half_copy(0, 1, s, pl.ds(HALF, W + AUG - HALF), rowb_s, rowb_r).wait_recv()

    def col_copy(src, dst, sem, where):
        return pltpu.make_async_remote_copy(
            src_ref=cols.at[src], dst_ref=cols.at[dst],
            send_sem=sem, recv_sem=col_r.at[dst], device_id=where, device_id_type=MESH)

    def sibling_copy(s):
        return col_copy(s, s + 1, sib_s.at[s // 2], line(1))

    def wait_col(s):
        col_copy(0, s, sib_s.at[0], line(1)).wait_recv()

    col_sends = [sibling_copy(0)]
    col_sends += [col_copy(0, line_back(s), col_s.at[s], line(s)) for s in (2, 4, 6, 8)]
    row_sends = [row_copy(s) for s in range(1, 7)]
    for cp in col_sends[:3] + row_sends + col_sends[3:]:
        cp.start()

    pass_on = {
        6: col_copy(6, 10, fwd_s.at[0], line(4)),
        8: col_copy(8, 12, fwd_s.at[1], line(2)),
        10: col_copy(10, 14, fwd_s.at[2], line(4)),
    }
    siblings = {s: sibling_copy(s) for s in range(2, 16, 2)}

    for s in (1, 2, 3, 4):
        row_in(s)
    wait_col(2)
    siblings[2].start()
    wait_col(4)
    siblings[4].start()
    wait_col(1)
    augment(1)
    augment(2)
    wait_col(3)
    augment(3)

    def col_in(s):
        wait_col(s)
        if s in pass_on:
            pass_on[s].start()
        siblings[s].start()

    events = {
        0: (lambda: row_in(5), lambda: row_in(6), lambda: col_in(6), lambda: wait_col(5)),
        1: (lambda: col_in(8), lambda: wait_col(7), lambda: halves_in(7)),
        2: (lambda: wait_col(9),),
        3: (lambda: col_in(10),),
        4: (lambda: col_in(12), lambda: wait_col(11)) + tuple(functools.partial(halves_in, s) for s in range(8, 12)),
        5: (lambda: col_in(14), lambda: wait_col(13)),
        6: (lambda: wait_col(15),) + tuple(functools.partial(halves_in, s) for s in range(12, 16)),
    }

    def reduce_copy(s):
        t = plane_back(s)
        return pltpu.make_async_remote_copy(
            src_ref=acc.at[s, pl.ds(0, KS)], dst_ref=recvp.at[t],
            send_sem=red_s.at[s], recv_sem=red_r.at[t], device_id=plane(s), device_id_type=MESH)

    red = {s: reduce_copy(s) for s in range(1, 16)}
    ones = jnp.where(lax.broadcasted_iota(jnp.int32, (KR - KC, G * B), 0) == 0, 1.0, 0.0).astype(jnp.bfloat16)

    def step(t, _):
        early = t < 4
        cg = jnp.where(t < 8, jnp.where(early, t // 2, t % 2), 2 + t % 2)
        rg = jnp.where(t < 8, jnp.where(early, t % 2, t // 2), 7 - t // 2)
        for k, todo in events.items():
            @pl.when(t == k)
            def _():
                for f in todo:
                    f()

        c0, r0 = cg * G, rg * G
        chunk = cols[pl.ds(c0, G)]
        lhs = jnp.concatenate(
            [chunk[:, :B].reshape(G * B, W), colaug[pl.ds(c0, G)].reshape(G * B, W)], axis=1)
        pt = jnp.concatenate(
            [chunk[k, B + h * KC:B + (h + 1) * KC] for k in range(G) for h in range(2)], axis=1)
        pt = jnp.concatenate([pt, ones], axis=0)
        rhs = jnp.concatenate([rows[r0 + k] for k in range(G)], axis=1)
        g = jnp.dot(lhs, rhs, preferred_element_type=jnp.float32)
        a = jnp.exp2(g * coef)
        eye = lax.broadcasted_iota(jnp.int32, (B, B), 0) == lax.broadcasted_iota(jnp.int32, (B, B), 1)
        first = jnp.where(eye & (t == 0), 0.0, a[:B, :B])
        a = jnp.concatenate([jnp.concatenate([first, a[:B, B:]], axis=1), a[B:]], axis=0)
        o = jnp.dot(pt, a.astype(jnp.bfloat16), preferred_element_type=jnp.float32)
        for k in range(G):
            acc[r0 + k] += o[:, k * B:(k + 1) * B]

        pair = jnp.where(t < 3, 4 + 2 * t, jnp.minimum(2 + 2 * t, 14))
        augment(pair)
        augment(pair + 1)

        for k in range(1, 4):
            @pl.when(t == 15 - 2 * k)
            def _():
                for s in range(4 * k, 4 * k + 4):
                    red[s].start()
        return 0

    lax.fori_loop(0, 16, step, 0)
    for s in range(1, 4):
        red[s].start()
    sums = acc[0, :KS, :]
    for s in range(15, 0, -1):
        red[plane_back(s)].wait_recv()
        sums = sums + recvp[s]
    walked = sums[:KC, :] / sums[KC:KC + 1, :]

    part = jnp.sum(walked * walked, axis=1, keepdims=True)
    diag = lax.broadcasted_iota(jnp.int32, (KC, 128), 0) == lax.broadcasted_iota(jnp.int32, (KC, 128), 1)
    flat = jnp.sum(jnp.where(diag, part, 0.0), axis=0, keepdims=True)

    def stage(k, flat, where, back, ss, rs):
        st_send[k] = jnp.broadcast_to(flat, (8, 128))
        cps = []
        for s in range(15, 0, -1):
            cp = pltpu.make_async_remote_copy(
                src_ref=st_send.at[k], dst_ref=st_recv.at[k, back(s)],
                send_sem=ss.at[s], recv_sem=rs.at[back(s)],
                device_id=where(s), device_id_type=MESH)
            cp.start()
            cps.append(cp)
        for cp in cps:
            cp.wait_recv()
        for s in range(1, 16):
            flat = flat + st_recv[k, s, 0:1, :]
        return flat, cps

    flat, c1 = stage(0, flat, plane, plane_back, a_s, a_r)
    flat, c2 = stage(1, flat, line, line_back, b_s, b_r)
    mean = jnp.sum(jnp.where(diag, jnp.broadcast_to(flat, (KC, 128)), 0.0), axis=1, keepdims=True) / total
    out_ref[...] = walked / jnp.sqrt(mean + 1e-6)

    for cp in row_sends + sum(row_pass.values(), []) + col_sends + list(siblings.values()) + list(pass_on.values()) + list(red.values()) + c1 + c2:
        cp.wait_send()


def per_device(total, points, spread, panel):
    dma = pltpu.SemaphoreType.DMA((16,))
    return pl.pallas_call(
        functools.partial(kernel, total),
        out_shape=jax.ShapeDtypeStruct((KC, B), jnp.float32),
        in_specs=[pl.BlockSpec(memory_space=pltpu.SMEM)] + [pl.BlockSpec(memory_space=pltpu.VMEM)] * 2,
        out_specs=pl.BlockSpec(memory_space=pltpu.VMEM),
        scratch_shapes=[
            pltpu.VMEM((16, 2 * W, B), jnp.bfloat16),
            pltpu.VMEM((16, MSG, W), jnp.bfloat16),
            pltpu.VMEM((16, B, W), jnp.bfloat16),
            pltpu.VMEM((16, KR, B), jnp.float32),
            pltpu.VMEM((16, KS, B), jnp.float32),
            pltpu.VMEM((2, 8, 128), jnp.float32),
            pltpu.VMEM((2, 16, 8, 128), jnp.float32),
        ] + [dma] * 16,
        compiler_params=pltpu.CompilerParams(
            collective_id=0, has_side_effects=True, vmem_limit_bytes=48 << 20),
        cost_estimate=pl.CostEstimate(flops=2 * 4096 * 4096 * 160, bytes_accessed=1 << 20, transcendentals=4096 * 4096),
        name="walk",
    )(spread, points, panel.T)


def solution(mesh):
    P = jax.sharding.PartitionSpec
    total = float(B * mesh.size)
    return jax.shard_map(
        functools.partial(per_device, total),
        mesh=mesh,
        in_specs=(P(("rowblk", "colblk"), None), P(), P(("rowblk", "colblk"), None)),
        out_specs=P(None, ("rowblk", "colblk")),
        check_vma=False,
    )
```

```python
import functools
import math

import jax
import jax.numpy as jnp
from jax import lax
from jax.experimental import pallas as pl
from jax.experimental.pallas import tpu as pltpu

MESH = pl.DeviceIdType.MESH
LOG2E = math.log2(math.e)
B = 256
W = 128
KC = 32
KR = 48
KS = 40
AUG = 16
G = 4
HALF = 80
MSG = B + 2 * KC

PLANE = (
    (0, 0), (0, 1), (0, 3), (1, 0), (3, 0), (0, 2), (2, 0), (1, 1),
    (1, 3), (3, 1), (3, 3), (1, 2), (2, 1), (2, 3), (3, 2), (2, 2),
)
LINE = (
    (0, 0), (0, 1), (1, 0), (7, 0), (1, 1), (7, 1), (2, 0), (6, 0),
    (2, 1), (6, 1), (3, 0), (5, 0), (3, 1), (5, 1), (4, 0), (4, 1),
)
NEAR_PLANE = (1, 2, 3, 4, 5, 6)
NEAR_LINE = (1, 2, 3, 6, 7)


def plane_back(s):
    dx, dy = PLANE[s]
    return PLANE.index(((4 - dx) % 4, (4 - dy) % 4))


def line_back(s):
    dz, dc = LINE[s]
    return LINE.index(((8 - dz) % 8, dc))


def three_terms(v):
    hi = v.astype(jnp.bfloat16).astype(jnp.float32)
    mid = (v - hi).astype(jnp.bfloat16).astype(jnp.float32)
    return hi, mid, v - hi - mid


def kernel(
    total,
    spread_ref, points_ref, panel_ref, out_ref,
    rows, cols, panel, colaug, acc, recvp, st_send, st_recv,
    row_s, row_r, rowa_s, rowa_r, rowb_s, rowb_r, col_s, col_r, sib_s, fwd_s, in_s, red_s, red_r, a_s, a_r, b_s, b_r,
):
    r = lax.axis_index("rowblk")
    c = lax.axis_index("colblk")
    z, xl = r // 2, r % 2
    xh, y, core = c // 8, (c // 2) % 4, c % 2
    x = xh * 2 + xl

    def dev(xx, yy, zz, cc):
        return {"rowblk": zz * 2 + xx % 2, "colblk": ((xx // 2) * 4 + yy) * 2 + cc}

    def plane(s):
        dx, dy = PLANE[s]
        return dev((x + dx) % 4, (y + dy) % 4, z, core)

    def line(s):
        dz, dc = LINE[s]
        return dev(x, y, (z + dz) % 8, (core + dc) % 2)

    barrier = pltpu.get_barrier_semaphore()
    for s in NEAR_LINE:
        pl.semaphore_signal(barrier, inc=1, device_id=line(s), device_id_type=MESH)
    for s in NEAR_PLANE:
        pl.semaphore_signal(barrier, inc=1, device_id=plane(s), device_id_type=MESH)

    fetch = [
        pltpu.make_async_copy(points_ref, cols.at[0, pl.ds(0, B)], in_s.at[0]),
        pltpu.make_async_copy(panel_ref, panel, in_s.at[1]),
    ]
    for cp in fetch:
        cp.start()

    def fill(s, _):
        rows[s, W + AUG:, :] = jnp.zeros((W - AUG, B), jnp.bfloat16)
        return 0
    lax.fori_loop(0, 16, fill, 0)
    acc[...] = jnp.zeros_like(acc)
    for cp in fetch:
        cp.wait()

    pts = cols[0, :B, :]
    ptst = pts.astype(jnp.float32).T
    hi, mid, lo = three_terms(-0.5 * jnp.sum(ptst * ptst, axis=0, keepdims=True))
    row = lax.broadcasted_iota(jnp.int32, (AUG, B), 0)
    aug = jnp.where(row == 0, hi, jnp.where(row == 1, mid, jnp.where(row == 2, lo, 0.0)))
    aug = jnp.where((row >= 3) & (row < 6), 1.0, aug)
    rows[0, :W, :] = ptst.astype(jnp.bfloat16)
    rows[0, W:W + AUG, :] = aug.astype(jnp.bfloat16)
    cols[0, B:B + KC, :] = panel[:, :W]
    cols[0, B + KC:, :] = panel[:, W:]

    coef = LOG2E / (spread_ref[0] * spread_ref[0])

    def augment(s):
        xf = cols[s, :B, :].astype(jnp.float32)
        jh, jm, jl = three_terms(-0.5 * jnp.sum(xf * xf, axis=1, keepdims=True))
        lane = lax.broadcasted_iota(jnp.int32, (B, W), 1)
        ja = jnp.where(lane == 3, jh, jnp.where(lane == 4, jm, jnp.where(lane == 5, jl, 0.0)))
        colaug[s] = jnp.where(lane < 3, 1.0, ja).astype(jnp.bfloat16)

    augment(0)

    pl.semaphore_wait(barrier, len(NEAR_LINE) + len(NEAR_PLANE))

    def row_copy(s):
        t = plane_back(s)
        return pltpu.make_async_remote_copy(
            src_ref=rows.at[0, pl.ds(0, W + AUG)], dst_ref=rows.at[t, pl.ds(0, W + AUG)],
            send_sem=row_s.at[s], recv_sem=row_r.at[t], device_id=plane(s), device_id_type=MESH)

    def half_copy(src, to, dst, part, ss, rs):
        return pltpu.make_async_remote_copy(
            src_ref=rows.at[src, part], dst_ref=rows.at[dst, part],
            send_sem=ss.at[dst], recv_sem=rs.at[dst], device_id=plane(to), device_id_type=MESH)

    row_pass = {}
    for e in (1, 3, 2):
        for d in (1, 3, 2):
            src, to = PLANE.index((0, d)), PLANE.index((e, 0))
            row_pass.setdefault(src, []).append(
                half_copy(src, to, PLANE.index(((4 - e) % 4, d)), pl.ds(0, HALF), rowa_s, rowa_r))
            src, to = PLANE.index((d, 0)), PLANE.index((0, e))
            row_pass.setdefault(src, []).append(
                half_copy(src, to, PLANE.index((d, (4 - e) % 4)), pl.ds(HALF, W + AUG - HALF), rowb_s, rowb_r))

    def row_in(s):
        row_copy(plane_back(s)).wait_recv()
        for cp in row_pass[s]:
            cp.start()

    def halves_in(s):
        half_copy(0, 1, s, pl.ds(0, HALF), rowa_s, rowa_r).wait_recv()
        half_copy(0, 1, s, pl.ds(HALF, W + AUG - HALF), rowb_s, rowb_r).wait_recv()

    def col_copy(src, dst, sem, where, part=pl.ds(0, MSG), arrival=None):
        return pltpu.make_async_remote_copy(
            src_ref=cols.at[src, part], dst_ref=cols.at[dst, part],
            send_sem=sem, recv_sem=col_r.at[dst if arrival is None else arrival], device_id=where, device_id_type=MESH)

    def wait_col(s):
        col_copy(0, s, sib_s.at[0], line(1)).wait_recv()

    at = LINE.index
    half = MSG // 2
    col_pass = {
        0: [
            col_copy(0, at((1, 0)), fwd_s.at[0], line(at((7, 0)))),
            col_copy(0, at((7, 0)), fwd_s.at[1], line(at((1, 0)))),
            col_copy(0, at((0, 1)), sib_s.at[0], line(1)),
            col_copy(0, at((2, 0)), fwd_s.at[2], line(at((6, 0)))),
            col_copy(0, at((6, 0)), fwd_s.at[3], line(at((2, 0)))),
        ],
        at((1, 0)): [], at((7, 0)): [],
        at((2, 0)): [
            col_copy(at((2, 0)), at((3, 0)), fwd_s.at[4], line(at((7, 0)))),
            col_copy(at((2, 0)), at((4, 0)), fwd_s.at[6], line(at((6, 0))), pl.ds(0, half)),
        ],
        at((6, 0)): [
            col_copy(at((6, 0)), at((5, 0)), fwd_s.at[5], line(at((1, 0)))),
            col_copy(at((6, 0)), at((4, 0)), fwd_s.at[7], line(at((2, 0))), pl.ds(half, half), 16),
        ],
        at((3, 0)): [], at((5, 0)): [], at((4, 0)): [],
    }
    for dz in range(1, 8):
        s = at((dz, 0))
        col_pass[s].append(col_copy(s, at((dz, 1)), sib_s.at[dz], line(1)))
    row_sends = [row_copy(s) for s in (1, 2, 3, 4, 5, 6)]

    def col_in(s):
        if LINE[s] == (4, 0):
            col_pass[at((2, 0))][1].wait_recv()
            col_pass[at((6, 0))][1].wait_recv()
        else:
            wait_col(s)
        for cp in col_pass[s]:
            cp.start()

    for cp in col_pass[0][:3] + row_sends[:4] + col_pass[0][3:] + row_sends[4:]:
        cp.start()

    col_in(2)
    col_in(3)
    for s in (1, 2, 3, 4):
        row_in(s)
    wait_col(1)
    for s in (1, 2, 3):
        augment(s)

    def pair_augment(s):
        augment(s)
        augment(s + 1)

    call = functools.partial
    events = {
        1: (call(row_in, 5), call(row_in, 6), call(wait_col, 4), call(wait_col, 5), call(col_in, 6), call(col_in, 7), call(halves_in, 7)),
        2: (call(pair_augment, 6),),
        4: (call(col_in, 10), call(col_in, 11)) + tuple(call(halves_in, s) for s in range(8, 12)),
        5: (call(wait_col, 8), call(wait_col, 9)),
        6: tuple(call(halves_in, s) for s in range(12, 16)) + (call(col_in, 14), call(wait_col, 12), call(wait_col, 13)),
        8: (call(wait_col, 15), ),
    }
    order = ((0, 0), (0, 1), (1, 0), (1, 1), (0, 2), (1, 2), (0, 3), (1, 3), (2, 3), (3, 3), (2, 2), (3, 2), (2, 1), (3, 1), (2, 0), (3, 0))
    complete = {9: 3, 11: 2, 13: 1}
    pairs = {1: 4, 4: 10, 5: 8, 6: 12, 8: 14}

    def choose(t, table):
        out = jnp.int32(0)
        for k, v in table.items():
            if v:
                out = jnp.where(t == k, v, out)
        return out

    def reduce_copy(s):
        t = plane_back(s)
        return pltpu.make_async_remote_copy(
            src_ref=acc.at[s, pl.ds(0, KS)], dst_ref=recvp.at[t, pl.ds(0, KS)],
            send_sem=red_s.at[s], recv_sem=red_r.at[t], device_id=plane(s), device_id_type=MESH)

    red = {s: reduce_copy(s) for s in range(1, 16)}
    ones = jnp.where(lax.broadcasted_iota(jnp.int32, (KR - KC, G * B), 0) == 0, 1.0, 0.0).astype(jnp.bfloat16)

    def step(t, _):
        cg = choose(t, {k: v[0] for k, v in enumerate(order)})
        rg = choose(t, {k: v[1] for k, v in enumerate(order)})
        for k, todo in events.items():
            @pl.when(t == k)
            def _():
                for f in todo:
                    f()

        c0, r0 = cg * G, rg * G
        chunk = cols[pl.ds(c0, G)]
        lhs = jnp.concatenate(
            [chunk[:, :B].reshape(G * B, W), colaug[pl.ds(c0, G)].reshape(G * B, W)], axis=1)
        pt = jnp.concatenate(
            [chunk[k, B + h * KC:B + (h + 1) * KC] for k in range(G) for h in range(2)], axis=1)
        pt = jnp.concatenate([pt, ones], axis=0)
        rhs = jnp.concatenate([rows[r0 + k] for k in range(G)], axis=1)
        g = jnp.dot(lhs, rhs, preferred_element_type=jnp.float32)
        a = jnp.exp2(g * coef)
        eye = lax.broadcasted_iota(jnp.int32, (B, B), 0) == lax.broadcasted_iota(jnp.int32, (B, B), 1)
        first = jnp.where(eye & (t == 0), 0.0, a[:B, :B])
        a = jnp.concatenate([jnp.concatenate([first, a[:B, B:]], axis=1), a[B:]], axis=0)
        o = jnp.dot(pt, a.astype(jnp.bfloat16), preferred_element_type=jnp.float32)
        for k in range(G):
            acc[r0 + k] += o[:, k * B:(k + 1) * B]

        pair = choose(t, pairs)
        augment(pair)
        augment(pair + 1)

        for k, q in complete.items():
            @pl.when(t == k)
            def _():
                for s in range(4 * q, 4 * q + 4):
                    red[s].start()
        return 0

    lax.fori_loop(0, 16, step, 0)
    for s in range(1, 4):
        red[s].start()
    sums = acc[0, :KS, :]
    for s in range(15, 0, -1):
        red[plane_back(s)].wait_recv()
        sums = sums + recvp[s, :KS]
    walked = sums[:KC, :] / sums[KC:KC + 1, :]

    part = jnp.sum(walked * walked, axis=1, keepdims=True)
    diag = lax.broadcasted_iota(jnp.int32, (KC, 128), 0) == lax.broadcasted_iota(jnp.int32, (KC, 128), 1)
    flat = jnp.sum(jnp.where(diag, part, 0.0), axis=0, keepdims=True)

    def stage(k, flat, where, back, ss, rs):
        st_send[k] = jnp.broadcast_to(flat, (8, 128))
        cps = []
        for s in range(15, 0, -1):
            cp = pltpu.make_async_remote_copy(
                src_ref=st_send.at[k], dst_ref=st_recv.at[k, back(s)],
                send_sem=ss.at[s], recv_sem=rs.at[back(s)],
                device_id=where(s), device_id_type=MESH)
            cp.start()
            cps.append(cp)
        for cp in cps:
            cp.wait_recv()
        for s in range(1, 16):
            flat = flat + st_recv[k, s, 0:1, :]
        return flat, cps

    flat, c1 = stage(0, flat, plane, plane_back, a_s, a_r)
    flat, c2 = stage(1, flat, line, line_back, b_s, b_r)
    mean = jnp.sum(jnp.where(diag, jnp.broadcast_to(flat, (KC, 128)), 0.0), axis=1, keepdims=True) / total
    out_ref[...] = walked / jnp.sqrt(mean + 1e-6)

    for cp in row_sends + sum(row_pass.values(), []) + sum(col_pass.values(), []) + list(red.values()) + c1 + c2:
        cp.wait_send()


def per_device(total, points, spread, panel):
    dma = pltpu.SemaphoreType.DMA((24,))
    return pl.pallas_call(
        functools.partial(kernel, total),
        out_shape=jax.ShapeDtypeStruct((KC, B), jnp.float32),
        in_specs=[pl.BlockSpec(memory_space=pltpu.SMEM)] + [pl.BlockSpec(memory_space=pltpu.HBM)] * 2,
        out_specs=pl.BlockSpec(memory_space=pltpu.VMEM),
        scratch_shapes=[
            pltpu.VMEM((16, 2 * W, B), jnp.bfloat16),
            pltpu.VMEM((16, MSG, W), jnp.bfloat16),
            pltpu.VMEM((KC, B), jnp.bfloat16),
            pltpu.VMEM((16, B, W), jnp.bfloat16),
            pltpu.VMEM((16, KR, B), jnp.float32),
            pltpu.VMEM((16, KR, B), jnp.float32),
            pltpu.VMEM((2, 8, 128), jnp.float32),
            pltpu.VMEM((2, 16, 8, 128), jnp.float32),
        ] + [dma] * 17,
        compiler_params=pltpu.CompilerParams(
            collective_id=0, has_side_effects=True, vmem_limit_bytes=48 << 20),
        cost_estimate=pl.CostEstimate(flops=2 * 4096 * 4096 * 160, bytes_accessed=1 << 20, transcendentals=4096 * 4096),
        name="walk",
    )(spread, points, panel.T)


def solution(mesh):
    P = jax.sharding.PartitionSpec
    total = float(B * mesh.size)
    return jax.shard_map(
        functools.partial(per_device, total),
        mesh=mesh,
        in_specs=(P(("rowblk", "colblk"), None), P(), P(("rowblk", "colblk"), None)),
        out_specs=P(None, ("rowblk", "colblk")),
        check_vma=False,
    )
```

```python
import functools
import math

import jax
import jax.numpy as jnp
from jax import lax
from jax.experimental import pallas as pl
from jax.experimental.pallas import tpu as pltpu

MESH = pl.DeviceIdType.MESH
LOG2E = math.log2(math.e)
B = 256
W = 128
KC = 32
KR = 48
KS = 40
AUG = 16
G = 4
HALF = 80
MSG = B + 2 * KC

PLANE = (
    (0, 0), (0, 1), (0, 3), (1, 0), (3, 0), (0, 2), (2, 0), (1, 1),
    (1, 3), (3, 1), (3, 3), (1, 2), (2, 1), (2, 3), (3, 2), (2, 2),
)
LINE = (
    (0, 0), (0, 1), (1, 0), (7, 0), (1, 1), (7, 1), (2, 0), (6, 0),
    (2, 1), (6, 1), (3, 0), (5, 0), (3, 1), (5, 1), (4, 0), (4, 1),
)
NEAR_PLANE = (1, 2, 3, 4, 5, 6)
NEAR_LINE = (1, 2, 3, 6, 7)


def plane_back(s):
    dx, dy = PLANE[s]
    return PLANE.index(((4 - dx) % 4, (4 - dy) % 4))


def line_back(s):
    dz, dc = LINE[s]
    return LINE.index(((8 - dz) % 8, dc))


def three_terms(v):
    hi = v.astype(jnp.bfloat16).astype(jnp.float32)
    mid = (v - hi).astype(jnp.bfloat16).astype(jnp.float32)
    return hi, mid, v - hi - mid


def kernel(
    total,
    spread_ref, points_ref, panel_ref, out_ref,
    rows, cols, panel, colaug, acc, recvp, st_send, st_recv,
    row_s, row_r, rowa_s, rowa_r, rowb_s, rowb_r, col_s, col_r, sib_s, fwd_s, in_s, red_s, red_r, a_s, a_r, b_s, b_r,
):
    r = lax.axis_index("rowblk")
    c = lax.axis_index("colblk")
    z, xl = r // 2, r % 2
    xh, y, core = c // 8, (c // 2) % 4, c % 2
    x = xh * 2 + xl

    def dev(xx, yy, zz, cc):
        return {"rowblk": zz * 2 + xx % 2, "colblk": ((xx // 2) * 4 + yy) * 2 + cc}

    def plane(s):
        dx, dy = PLANE[s]
        return dev((x + dx) % 4, (y + dy) % 4, z, core)

    def line(s):
        dz, dc = LINE[s]
        return dev(x, y, (z + dz) % 8, (core + dc) % 2)

    barrier = pltpu.get_barrier_semaphore()
    for s in NEAR_LINE:
        pl.semaphore_signal(barrier, inc=1, device_id=line(s), device_id_type=MESH)
    for s in NEAR_PLANE:
        pl.semaphore_signal(barrier, inc=1, device_id=plane(s), device_id_type=MESH)

    fetch = [
        pltpu.make_async_copy(points_ref, cols.at[0, pl.ds(0, B)], in_s.at[0]),
        pltpu.make_async_copy(panel_ref, panel, in_s.at[1]),
    ]
    for cp in fetch:
        cp.start()

    def fill(s, _):
        rows[s, W + AUG:, :] = jnp.zeros((W - AUG, B), jnp.bfloat16)
        return 0
    lax.fori_loop(0, 16, fill, 0)
    acc[...] = jnp.zeros_like(acc)
    for cp in fetch:
        cp.wait()

    pts = cols[0, :B, :]
    ptst = pts.astype(jnp.float32).T
    hi, mid, lo = three_terms(-0.5 * jnp.sum(ptst * ptst, axis=0, keepdims=True))
    row = lax.broadcasted_iota(jnp.int32, (AUG, B), 0)
    aug = jnp.where(row == 0, hi, jnp.where(row == 1, mid, jnp.where(row == 2, lo, 0.0)))
    aug = jnp.where((row >= 3) & (row < 6), 1.0, aug)
    rows[0, :W, :] = ptst.astype(jnp.bfloat16)
    rows[0, W:W + AUG, :] = aug.astype(jnp.bfloat16)
    cols[0, B:B + KC, :] = panel[:, :W]
    cols[0, B + KC:, :] = panel[:, W:]

    coef = LOG2E / (spread_ref[0] * spread_ref[0])

    def augment(s):
        xf = cols[s, :B, :].astype(jnp.float32)
        jh, jm, jl = three_terms(-0.5 * jnp.sum(xf * xf, axis=1, keepdims=True))
        lane = lax.broadcasted_iota(jnp.int32, (B, W), 1)
        ja = jnp.where(lane == 3, jh, jnp.where(lane == 4, jm, jnp.where(lane == 5, jl, 0.0)))
        colaug[s] = jnp.where(lane < 3, 1.0, ja).astype(jnp.bfloat16)

    augment(0)

    pl.semaphore_wait(barrier, len(NEAR_LINE) + len(NEAR_PLANE))

    def row_copy(s):
        t = plane_back(s)
        return pltpu.make_async_remote_copy(
            src_ref=rows.at[0, pl.ds(0, W + AUG)], dst_ref=rows.at[t, pl.ds(0, W + AUG)],
            send_sem=row_s.at[s], recv_sem=row_r.at[t], device_id=plane(s), device_id_type=MESH)

    def half_copy(src, to, dst, part, ss, rs):
        return pltpu.make_async_remote_copy(
            src_ref=rows.at[src, part], dst_ref=rows.at[dst, part],
            send_sem=ss.at[dst], recv_sem=rs.at[dst], device_id=plane(to), device_id_type=MESH)

    row_pass = {}
    for e in (1, 3, 2):
        for d in (1, 3, 2):
            src, to = PLANE.index((0, d)), PLANE.index((e, 0))
            row_pass.setdefault(src, []).append(
                half_copy(src, to, PLANE.index(((4 - e) % 4, d)), pl.ds(0, HALF), rowa_s, rowa_r))
            src, to = PLANE.index((d, 0)), PLANE.index((0, e))
            row_pass.setdefault(src, []).append(
                half_copy(src, to, PLANE.index((d, (4 - e) % 4)), pl.ds(HALF, W + AUG - HALF), rowb_s, rowb_r))

    def row_in(s):
        row_copy(plane_back(s)).wait_recv()
        for cp in row_pass[s]:
            cp.start()

    def halves_in(s):
        half_copy(0, 1, s, pl.ds(0, HALF), rowa_s, rowa_r).wait_recv()
        half_copy(0, 1, s, pl.ds(HALF, W + AUG - HALF), rowb_s, rowb_r).wait_recv()

    def col_copy(src, dst, sem, where, part=pl.ds(0, MSG), arrival=None):
        return pltpu.make_async_remote_copy(
            src_ref=cols.at[src, part], dst_ref=cols.at[dst, part],
            send_sem=sem, recv_sem=col_r.at[dst if arrival is None else arrival], device_id=where, device_id_type=MESH)

    def wait_col(s):
        col_copy(0, s, sib_s.at[0], line(1)).wait_recv()

    at = LINE.index
    half = MSG // 2
    col_pass = {
        0: [
            col_copy(0, at((1, 0)), fwd_s.at[0], line(at((7, 0)))),
            col_copy(0, at((7, 0)), fwd_s.at[1], line(at((1, 0)))),
            col_copy(0, at((0, 1)), sib_s.at[0], line(1)),
            col_copy(0, at((2, 0)), fwd_s.at[2], line(at((6, 0)))),
            col_copy(0, at((6, 0)), fwd_s.at[3], line(at((2, 0)))),
        ],
        at((1, 0)): [], at((7, 0)): [],
        at((2, 0)): [
            col_copy(at((2, 0)), at((3, 0)), fwd_s.at[4], line(at((7, 0)))),
            col_copy(at((2, 0)), at((4, 0)), fwd_s.at[6], line(at((6, 0))), pl.ds(0, half)),
        ],
        at((6, 0)): [
            col_copy(at((6, 0)), at((5, 0)), fwd_s.at[5], line(at((1, 0)))),
            col_copy(at((6, 0)), at((4, 0)), fwd_s.at[7], line(at((2, 0))), pl.ds(half, half), 16),
        ],
        at((3, 0)): [], at((5, 0)): [], at((4, 0)): [],
    }
    for dz in range(1, 8):
        s = at((dz, 0))
        col_pass[s].append(col_copy(s, at((dz, 1)), sib_s.at[dz], line(1)))
    row_sends = [row_copy(s) for s in (1, 2, 3, 4, 5, 6)]

    def col_in(s):
        if LINE[s] == (4, 0):
            col_pass[at((2, 0))][1].wait_recv()
            col_pass[at((6, 0))][1].wait_recv()
        else:
            wait_col(s)
        for cp in col_pass[s]:
            cp.start()

    for cp in col_pass[0][:3] + row_sends[:4] + col_pass[0][3:] + row_sends[4:]:
        cp.start()

    col_in(2)
    col_in(3)
    for s in (1, 2, 3, 4):
        row_in(s)
    wait_col(1)
    for s in (1, 2, 3):
        augment(s)

    ones = jnp.where(lax.broadcasted_iota(jnp.int32, (KR - KC, 8 * B), 0) == 0, 1.0, 0.0).astype(jnp.bfloat16)

    def chunk(c0, nc, r0, nr, own=False):
        part = cols[pl.ds(c0, nc)]
        lhs = jnp.concatenate(
            [part[:, :B].reshape(nc * B, W), colaug[pl.ds(c0, nc)].reshape(nc * B, W)], axis=1)
        pt = jnp.concatenate(
            [part[k, B + h * KC:B + (h + 1) * KC] for k in range(nc) for h in range(2)], axis=1)
        pt = jnp.concatenate([pt, ones[:, :nc * B]], axis=0)
        rhs = jnp.concatenate([rows[r0 + k] for k in range(nr)], axis=1)
        g = jnp.dot(lhs, rhs, preferred_element_type=jnp.float32)
        a = jnp.exp2(g * coef)
        if own:
            eye = lax.broadcasted_iota(jnp.int32, (B, B), 0) == lax.broadcasted_iota(jnp.int32, (B, B), 1)
            first = jnp.where(eye, 0.0, a[:B, :B])
            a = jnp.concatenate([jnp.concatenate([first, a[:B, B:]], axis=1), a[B:]], axis=0)
        o = jnp.dot(pt, a.astype(jnp.bfloat16), preferred_element_type=jnp.float32)
        for k in range(nr):
            acc[r0 + k] += o[:, k * B:(k + 1) * B]

    chunk(0, 4, 0, 4, own=True)
    row_in(5)
    row_in(6)
    chunk(0, 4, 4, 3)
    wait_col(4)
    wait_col(5)
    augment(4)
    augment(5)
    chunk(4, 2, 0, 7)
    col_in(6)
    col_in(7)
    augment(6)
    augment(7)
    chunk(6, 2, 0, 7)
    halves_in(7)
    chunk(0, 8, 7, 1)

    call = functools.partial
    events = {
        0: tuple(call(halves_in, s) for s in range(8, 12)),
        1: (call(col_in, 10), call(col_in, 11), call(wait_col, 8), call(wait_col, 9)) + tuple(call(halves_in, s) for s in range(12, 16)),
        2: (call(col_in, 14), call(wait_col, 12), call(wait_col, 13), call(augment, 12), call(augment, 13), call(augment, 14),
            call(wait_col, 15), call(augment, 15)),
    }
    order = ((0, 2), (0, 3), (8, 3), (8, 2), (8, 1), (8, 0))
    complete = {2: 3, 3: 2, 4: 1}

    def choose(t, table):
        out = jnp.int32(0)
        for k, v in table.items():
            if v:
                out = jnp.where(t == k, v, out)
        return out

    def reduce_copy(s):
        t = plane_back(s)
        return pltpu.make_async_remote_copy(
            src_ref=acc.at[s, pl.ds(0, KS)], dst_ref=recvp.at[t, pl.ds(0, KS)],
            send_sem=red_s.at[s], recv_sem=red_r.at[t], device_id=plane(s), device_id_type=MESH)

    red = {s: reduce_copy(s) for s in range(1, 16)}
    def step(t, _):
        c0 = choose(t, {k: v[0] for k, v in enumerate(order)})
        r0 = G * choose(t, {k: v[1] for k, v in enumerate(order)})
        for k, todo in events.items():
            @pl.when(t == k)
            def _():
                for f in todo:
                    f()

        chunk(c0, 8, r0, G)
        for k in range(4):
            augment(jnp.where(t == 0, 0, 8) + k)

        for k, q in complete.items():
            @pl.when(t == k)
            def _():
                for s in range(4 * q, 4 * q + 4):
                    red[s].start()
        return 0

    lax.fori_loop(0, 6, step, 0)
    for s in range(1, 4):
        red[s].start()
    for cp in row_sends + sum(row_pass.values(), []) + sum(col_pass.values(), []):
        cp.wait_send()
    sums = acc[0, :KS, :]
    for s in range(15, 0, -1):
        red[plane_back(s)].wait_recv()
        sums = sums + recvp[s, :KS]
    walked = sums[:KC, :] / sums[KC:KC + 1, :]

    part = jnp.sum(walked * walked, axis=1, keepdims=True)
    diag = lax.broadcasted_iota(jnp.int32, (KC, 128), 0) == lax.broadcasted_iota(jnp.int32, (KC, 128), 1)
    flat = jnp.sum(jnp.where(diag, part, 0.0), axis=0, keepdims=True)

    def stage(k, flat, where, back, ss, rs, before):
        st_send[k] = jnp.broadcast_to(flat, (8, 128))
        cps = []
        for s in range(15, 0, -1):
            cp = pltpu.make_async_remote_copy(
                src_ref=st_send.at[k], dst_ref=st_recv.at[k, back(s)],
                send_sem=ss.at[s], recv_sem=rs.at[back(s)],
                device_id=where(s), device_id_type=MESH)
            cp.start()
            cps.append(cp)
        for cp in before:
            cp.wait_send()
        for cp in cps:
            cp.wait_recv()
        for s in range(1, 16):
            flat = flat + st_recv[k, s, 0:1, :]
        return flat, cps

    flat, c1 = stage(0, flat, plane, plane_back, a_s, a_r, list(red.values()))
    flat, c2 = stage(1, flat, line, line_back, b_s, b_r, c1)
    mean = jnp.sum(jnp.where(diag, jnp.broadcast_to(flat, (KC, 128)), 0.0), axis=1, keepdims=True) / total
    out_ref[...] = walked / jnp.sqrt(mean + 1e-6)

    for cp in c2:
        cp.wait_send()


def per_device(total, points, spread, panel):
    dma = pltpu.SemaphoreType.DMA((24,))
    return pl.pallas_call(
        functools.partial(kernel, total),
        out_shape=jax.ShapeDtypeStruct((KC, B), jnp.float32),
        in_specs=[pl.BlockSpec(memory_space=pltpu.SMEM)] + [pl.BlockSpec(memory_space=pltpu.HBM)] * 2,
        out_specs=pl.BlockSpec(memory_space=pltpu.VMEM),
        scratch_shapes=[
            pltpu.VMEM((16, 2 * W, B), jnp.bfloat16),
            pltpu.VMEM((16, MSG, W), jnp.bfloat16),
            pltpu.VMEM((KC, B), jnp.bfloat16),
            pltpu.VMEM((16, B, W), jnp.bfloat16),
            pltpu.VMEM((16, KR, B), jnp.float32),
            pltpu.VMEM((16, KR, B), jnp.float32),
            pltpu.VMEM((2, 8, 128), jnp.float32),
            pltpu.VMEM((2, 16, 8, 128), jnp.float32),
        ] + [dma] * 17,
        compiler_params=pltpu.CompilerParams(
            collective_id=0, has_side_effects=True, vmem_limit_bytes=48 << 20),
        cost_estimate=pl.CostEstimate(flops=2 * 4096 * 4096 * 160, bytes_accessed=1 << 20, transcendentals=4096 * 4096),
        name="walk",
    )(spread, pltpu.with_memory_space_constraint(points, pltpu.HBM), pltpu.with_memory_space_constraint(panel.T, pltpu.HBM))


def solution(mesh):
    P = jax.sharding.PartitionSpec
    total = float(B * mesh.size)
    return jax.shard_map(
        functools.partial(per_device, total),
        mesh=mesh,
        in_specs=(P(("rowblk", "colblk"), None), P(), P(("rowblk", "colblk"), None)),
        out_specs=P(None, ("rowblk", "colblk")),
        check_vma=False,
    )
```

```python
import functools
import math

import jax
import jax.numpy as jnp
from jax import lax
from jax.experimental import pallas as pl
from jax.experimental.pallas import tpu as pltpu

MESH = pl.DeviceIdType.MESH
LOG2E = math.log2(math.e)
B = 256
W = 128
KC = 32
KR = 48
L = 128
KS = 2 * KC + 8
AUG = 16
G = 4
HALF = 80
MSG = B + 2 * KC

PLANE = (
    (0, 0), (0, 1), (0, 3), (1, 0), (3, 0), (0, 2), (2, 0), (1, 1),
    (1, 3), (3, 1), (3, 3), (1, 2), (2, 1), (2, 3), (3, 2), (2, 2),
)
LINE = (
    (0, 0), (0, 1), (1, 0), (7, 0), (1, 1), (7, 1), (2, 0), (6, 0),
    (2, 1), (6, 1), (3, 0), (5, 0), (3, 1), (5, 1), (4, 0), (4, 1),
)
NEAR_PLANE = (1, 2, 3, 4, 5, 6)
NEAR_LINE = (1, 2, 3, 6, 7)


def plane_back(s):
    dx, dy = PLANE[s]
    return PLANE.index(((4 - dx) % 4, (4 - dy) % 4))


def line_back(s):
    dz, dc = LINE[s]
    return LINE.index(((8 - dz) % 8, dc))


def three_terms(v):
    hi = v.astype(jnp.bfloat16).astype(jnp.float32)
    mid = (v - hi).astype(jnp.bfloat16).astype(jnp.float32)
    return hi, mid, v - hi - mid


def kernel(
    total,
    spread_ref, points_ref, panel_ref, out_ref,
    rows, cols, panel, colaug, acc, recvp, st_send, st_recv,
    row_s, row_r, rowa_s, rowa_r, rowb_s, rowb_r, col_s, col_r, sib_s, fwd_s, in_s, red_s, red_r, a_s, a_r, b_s, b_r,
):
    r = lax.axis_index("rowblk")
    c = lax.axis_index("colblk")
    z, xl = r // 2, r % 2
    xh, y, core = c // 8, (c // 2) % 4, c % 2
    x = xh * 2 + xl

    def dev(xx, yy, zz, cc):
        return {"rowblk": zz * 2 + xx % 2, "colblk": ((xx // 2) * 4 + yy) * 2 + cc}

    def plane(s):
        dx, dy = PLANE[s]
        return dev((x + dx) % 4, (y + dy) % 4, z, core)

    def line(s):
        dz, dc = LINE[s]
        return dev(x, y, (z + dz) % 8, (core + dc) % 2)

    barrier = pltpu.get_barrier_semaphore()
    for s in NEAR_LINE:
        pl.semaphore_signal(barrier, inc=1, device_id=line(s), device_id_type=MESH)
    for s in NEAR_PLANE:
        pl.semaphore_signal(barrier, inc=1, device_id=plane(s), device_id_type=MESH)

    fetch = [
        pltpu.make_async_copy(points_ref, cols.at[0, pl.ds(0, B)], in_s.at[0]),
        pltpu.make_async_copy(panel_ref, panel, in_s.at[1]),
    ]
    for cp in fetch:
        cp.start()

    def fill(s, _):
        rows[s, W + AUG:, :] = jnp.zeros((W - AUG, B), jnp.bfloat16)
        return 0
    lax.fori_loop(0, 16, fill, 0)
    acc[...] = jnp.zeros_like(acc)
    for cp in fetch:
        cp.wait()

    pts = cols[0, :B, :]
    ptst = pts.astype(jnp.float32).T
    hi, mid, lo = three_terms(-0.5 * jnp.sum(ptst * ptst, axis=0, keepdims=True))
    row = lax.broadcasted_iota(jnp.int32, (AUG, B), 0)
    aug = jnp.where(row == 0, hi, jnp.where(row == 1, mid, jnp.where(row == 2, lo, 0.0)))
    aug = jnp.where((row >= 3) & (row < 6), 1.0, aug)
    rows[0, :W, :] = ptst.astype(jnp.bfloat16)
    rows[0, W:W + AUG, :] = aug.astype(jnp.bfloat16)
    cols[0, B:B + KC, :] = panel[:, :W]
    cols[0, B + KC:, :] = panel[:, W:]

    coef = LOG2E / (spread_ref[0] * spread_ref[0])

    def augment(s):
        xf = cols[s, :B, :].astype(jnp.float32)
        jh, jm, jl = three_terms(-0.5 * jnp.sum(xf * xf, axis=1, keepdims=True))
        lane = lax.broadcasted_iota(jnp.int32, (B, W), 1)
        ja = jnp.where(lane == 3, jh, jnp.where(lane == 4, jm, jnp.where(lane == 5, jl, 0.0)))
        colaug[s] = jnp.where(lane < 3, 1.0, ja).astype(jnp.bfloat16)

    augment(0)

    pl.semaphore_wait(barrier, len(NEAR_LINE) + len(NEAR_PLANE))

    def row_copy(s):
        t = plane_back(s)
        return pltpu.make_async_remote_copy(
            src_ref=rows.at[0, pl.ds(0, W + AUG)], dst_ref=rows.at[t, pl.ds(0, W + AUG)],
            send_sem=row_s.at[s], recv_sem=row_r.at[t], device_id=plane(s), device_id_type=MESH)

    def half_copy(src, to, dst, part, ss, rs):
        return pltpu.make_async_remote_copy(
            src_ref=rows.at[src, part], dst_ref=rows.at[dst, part],
            send_sem=ss.at[dst], recv_sem=rs.at[dst], device_id=plane(to), device_id_type=MESH)

    row_pass = {}
    for e in (1, 3, 2):
        for d in (1, 3, 2):
            src, to = PLANE.index((0, d)), PLANE.index((e, 0))
            row_pass.setdefault(src, []).append(
                half_copy(src, to, PLANE.index(((4 - e) % 4, d)), pl.ds(0, HALF), rowa_s, rowa_r))
            src, to = PLANE.index((d, 0)), PLANE.index((0, e))
            row_pass.setdefault(src, []).append(
                half_copy(src, to, PLANE.index((d, (4 - e) % 4)), pl.ds(HALF, W + AUG - HALF), rowb_s, rowb_r))

    def row_in(s):
        row_copy(plane_back(s)).wait_recv()
        for cp in row_pass[s]:
            cp.start()

    def halves_in(s):
        half_copy(0, 1, s, pl.ds(0, HALF), rowa_s, rowa_r).wait_recv()
        half_copy(0, 1, s, pl.ds(HALF, W + AUG - HALF), rowb_s, rowb_r).wait_recv()

    def col_copy(src, dst, sem, where, part=pl.ds(0, MSG), arrival=None):
        return pltpu.make_async_remote_copy(
            src_ref=cols.at[src, part], dst_ref=cols.at[dst, part],
            send_sem=sem, recv_sem=col_r.at[dst if arrival is None else arrival], device_id=where, device_id_type=MESH)

    def wait_col(s):
        col_copy(0, s, sib_s.at[0], line(1)).wait_recv()

    at = LINE.index
    half = MSG // 2
    col_pass = {
        0: [
            col_copy(0, at((1, 0)), fwd_s.at[0], line(at((7, 0)))),
            col_copy(0, at((7, 0)), fwd_s.at[1], line(at((1, 0)))),
            col_copy(0, at((0, 1)), sib_s.at[0], line(1)),
            col_copy(0, at((2, 0)), fwd_s.at[2], line(at((6, 0)))),
            col_copy(0, at((6, 0)), fwd_s.at[3], line(at((2, 0)))),
        ],
        at((1, 0)): [], at((7, 0)): [],
        at((2, 0)): [
            col_copy(at((2, 0)), at((3, 0)), fwd_s.at[4], line(at((7, 0)))),
            col_copy(at((2, 0)), at((4, 0)), fwd_s.at[6], line(at((6, 0))), pl.ds(0, half)),
        ],
        at((6, 0)): [
            col_copy(at((6, 0)), at((5, 0)), fwd_s.at[5], line(at((1, 0)))),
            col_copy(at((6, 0)), at((4, 0)), fwd_s.at[7], line(at((2, 0))), pl.ds(half, half), 16),
        ],
        at((3, 0)): [], at((5, 0)): [], at((4, 0)): [],
    }
    for dz in range(1, 8):
        s = at((dz, 0))
        col_pass[s].append(col_copy(s, at((dz, 1)), sib_s.at[dz], line(1)))
    row_sends = [row_copy(s) for s in (1, 2, 3, 4, 5, 6)]

    def col_in(s):
        if LINE[s] == (4, 0):
            col_pass[at((2, 0))][1].wait_recv()
            col_pass[at((6, 0))][1].wait_recv()
        else:
            wait_col(s)
        for cp in col_pass[s]:
            cp.start()

    for cp in col_pass[0][:3] + row_sends[:4] + col_pass[0][3:] + row_sends[4:]:
        cp.start()

    col_in(2)
    col_in(3)
    for s in (1, 2, 3, 4):
        row_in(s)
    wait_col(1)
    for s in (1, 2, 3):
        augment(s)

    ones = jnp.where(lax.broadcasted_iota(jnp.int32, (KR - KC, 16 * B), 0) < 2, 1.0, 0.0).astype(jnp.bfloat16)

    upper = lax.broadcasted_iota(jnp.int32, (8, L), 0) == 0

    def chunk(c0, nc, r0, nr, own=False):
        part = cols[pl.ds(c0, nc)]
        lhs = jnp.concatenate(
            [part[:, :B].reshape(nc * B, W), colaug[pl.ds(c0, nc)].reshape(nc * B, W)], axis=1)
        pt = jnp.concatenate(
            [part[k, B + h * KC:B + (h + 1) * KC] for k in range(nc) for h in range(2)], axis=1)
        pt = jnp.concatenate([pt, ones[:, :nc * B]], axis=0)
        rhs = jnp.concatenate([rows[r0 + k] for k in range(nr)], axis=1)
        g = jnp.dot(lhs, rhs, preferred_element_type=jnp.float32)
        a = jnp.exp2(g * coef)
        if own:
            eye = lax.broadcasted_iota(jnp.int32, (B, B), 0) == lax.broadcasted_iota(jnp.int32, (B, B), 1)
            first = jnp.where(eye, 0.0, a[:B])
            a = jnp.concatenate([first, a[B:]], axis=0)
        o = jnp.dot(pt, a.astype(jnp.bfloat16), preferred_element_type=jnp.float32)
        for k in range(nr):
            left, right = o[:, k * B:k * B + L], o[:, k * B + L:(k + 1) * B]
            acc[r0 + k, :KC] += left[:KC]
            acc[r0 + k, KC:2 * KC] += right[:KC]
            acc[r0 + k, 2 * KC:] += jnp.where(upper, left[KC:KC + 8], right[KC:KC + 8])

    chunk(0, 4, 1, 4)
    row_in(5)
    row_in(6)
    chunk(0, 4, 5, 2)
    wait_col(4)
    wait_col(5)
    augment(4)
    augment(5)
    chunk(4, 2, 1, 6)
    col_in(6)
    col_in(7)
    augment(6)
    augment(7)
    chunk(6, 2, 1, 6)
    def reduce_copy(s):
        t = plane_back(s)
        return pltpu.make_async_remote_copy(
            src_ref=acc.at[s], dst_ref=recvp.at[t],
            send_sem=red_s.at[s], recv_sem=red_r.at[t], device_id=plane(s), device_id_type=MESH)

    red = {s: reduce_copy(s) for s in range(1, 16)}

    def send_sums(slots):
        for s in slots:
            red[s].start()

    for s in range(8, 12):
        halves_in(s)
    chunk(0, 8, 8, 4)
    col_in(10)
    col_in(11)
    for s in range(12, 16):
        halves_in(s)
    wait_col(8)
    wait_col(9)
    for s in range(8, 12):
        augment(s)
    chunk(0, 8, 12, 4)
    col_in(14)
    wait_col(12)
    wait_col(13)
    for s in range(12, 15):
        augment(s)
    chunk(8, 4, 12, 4)
    wait_col(15)
    augment(15)
    chunk(12, 4, 12, 4)
    send_sums(range(12, 16))
    chunk(8, 8, 8, 4)
    send_sums(range(8, 12))
    halves_in(7)
    chunk(0, 8, 7, 1)
    chunk(8, 8, 4, 4)
    send_sums(range(4, 8))
    chunk(8, 8, 1, 3)
    send_sums(range(1, 4))
    chunk(0, 16, 0, 1, own=True)
    for cp in row_sends + sum(row_pass.values(), []) + sum(col_pass.values(), []):
        cp.wait_send()
    sums = acc[0]
    for s in range(15, 0, -1):
        red[plane_back(s)].wait_recv()
        sums = sums + recvp[s]
    walked = [sums[h * KC:(h + 1) * KC] / sums[2 * KC + h:2 * KC + h + 1] for h in range(2)]

    part = jnp.sum(walked[0] * walked[0] + walked[1] * walked[1], axis=1, keepdims=True)
    diag = lax.broadcasted_iota(jnp.int32, (KC, 128), 0) == lax.broadcasted_iota(jnp.int32, (KC, 128), 1)
    flat = jnp.sum(jnp.where(diag, part, 0.0), axis=0, keepdims=True)

    def stage(k, flat, where, back, ss, rs, before):
        st_send[k] = jnp.broadcast_to(flat, (8, 128))
        cps = []
        for s in range(15, 0, -1):
            cp = pltpu.make_async_remote_copy(
                src_ref=st_send.at[k], dst_ref=st_recv.at[k, back(s)],
                send_sem=ss.at[s], recv_sem=rs.at[back(s)],
                device_id=where(s), device_id_type=MESH)
            cp.start()
            cps.append(cp)
        for cp in before:
            cp.wait_send()
        for cp in cps:
            cp.wait_recv()
        for s in range(1, 16):
            flat = flat + st_recv[k, s, 0:1, :]
        return flat, cps

    flat, c1 = stage(0, flat, plane, plane_back, a_s, a_r, list(red.values()))
    flat, c2 = stage(1, flat, line, line_back, b_s, b_r, c1)
    mean = jnp.sum(jnp.where(diag, jnp.broadcast_to(flat, (KC, 128)), 0.0), axis=1, keepdims=True) / total
    scale = jnp.sqrt(mean + 1e-6)
    for h in range(2):
        out_ref[:, h * L:(h + 1) * L] = walked[h] / scale

    for cp in c2:
        cp.wait_send()


def per_device(total, points, spread, panel):
    dma = pltpu.SemaphoreType.DMA((24,))
    return pl.pallas_call(
        functools.partial(kernel, total),
        out_shape=jax.ShapeDtypeStruct((KC, B), jnp.float32),
        in_specs=[pl.BlockSpec(memory_space=pltpu.SMEM)] + [pl.BlockSpec(memory_space=pltpu.HBM)] * 2,
        out_specs=pl.BlockSpec(memory_space=pltpu.VMEM),
        scratch_shapes=[
            pltpu.VMEM((16, 2 * W, B), jnp.bfloat16),
            pltpu.VMEM((16, MSG, W), jnp.bfloat16),
            pltpu.VMEM((KC, B), jnp.bfloat16),
            pltpu.VMEM((16, B, W), jnp.bfloat16),
            pltpu.VMEM((16, KS, L), jnp.float32),
            pltpu.VMEM((16, KS, L), jnp.float32),
            pltpu.VMEM((2, 8, 128), jnp.float32),
            pltpu.VMEM((2, 16, 8, 128), jnp.float32),
        ] + [dma] * 17,
        compiler_params=pltpu.CompilerParams(
            collective_id=0, has_side_effects=True, vmem_limit_bytes=48 << 20),
        cost_estimate=pl.CostEstimate(flops=2 * 4096 * 4096 * 160, bytes_accessed=1 << 20, transcendentals=4096 * 4096),
        name="walk",
    )(spread, pltpu.with_memory_space_constraint(points, pltpu.HBM), pltpu.with_memory_space_constraint(panel.T, pltpu.HBM))


def solution(mesh):
    P = jax.sharding.PartitionSpec
    total = float(B * mesh.size)
    return jax.shard_map(
        functools.partial(per_device, total),
        mesh=mesh,
        in_specs=(P(("rowblk", "colblk"), None), P(), P(("rowblk", "colblk"), None)),
        out_specs=P(None, ("rowblk", "colblk")),
        check_vma=False,
    )
```

```python
import functools
import math

import jax
import jax.numpy as jnp
from jax import lax
from jax.experimental import pallas as pl
from jax.experimental.pallas import tpu as pltpu

MESH = pl.DeviceIdType.MESH
LOG2E = math.log2(math.e)
B = 256
W = 128
KC = 32
KR = 48
L = 128
KS = 2 * KC + 8
AUG = 16
G = 4
HALF = 80
MSG = B + 2 * KC

PLANE = (
    (0, 0), (0, 1), (0, 3), (1, 0), (3, 0), (0, 2), (2, 0), (1, 1),
    (1, 3), (3, 1), (3, 3), (1, 2), (2, 1), (2, 3), (3, 2), (2, 2),
)
LINE = (
    (0, 0), (0, 1), (1, 0), (7, 0), (1, 1), (7, 1), (2, 0), (6, 0),
    (2, 1), (6, 1), (3, 0), (5, 0), (3, 1), (5, 1), (4, 0), (4, 1),
)
NEAR_PLANE = (1, 2, 3, 4, 5, 6)
NEAR_LINE = (1, 2, 3, 6, 7)


def plane_back(s):
    dx, dy = PLANE[s]
    return PLANE.index(((4 - dx) % 4, (4 - dy) % 4))


def line_back(s):
    dz, dc = LINE[s]
    return LINE.index(((8 - dz) % 8, dc))


def three_terms(v):
    hi = v.astype(jnp.bfloat16).astype(jnp.float32)
    mid = (v - hi).astype(jnp.bfloat16).astype(jnp.float32)
    return hi, mid, v - hi - mid


def kernel(
    total,
    spread_ref, points_ref, panel_ref, out_ref,
    rows, cols, panel, colaug, acc, recvp, st_send, st_recv,
    row_s, row_r, rowa_s, rowa_r, rowb_s, rowb_r, col_s, col_r, sib_s, fwd_s, in_s, red_s, red_r, a_s, a_r, b_s, b_r,
):
    r = lax.axis_index("rowblk")
    c = lax.axis_index("colblk")
    z, xl = r // 2, r % 2
    xh, y, core = c // 8, (c // 2) % 4, c % 2
    x = xh * 2 + xl

    def dev(xx, yy, zz, cc):
        return {"rowblk": zz * 2 + xx % 2, "colblk": ((xx // 2) * 4 + yy) * 2 + cc}

    def plane(s):
        dx, dy = PLANE[s]
        return dev((x + dx) % 4, (y + dy) % 4, z, core)

    def line(s):
        dz, dc = LINE[s]
        return dev(x, y, (z + dz) % 8, (core + dc) % 2)

    barrier = pltpu.get_barrier_semaphore()
    for s in NEAR_LINE:
        pl.semaphore_signal(barrier, inc=1, device_id=line(s), device_id_type=MESH)
    for s in NEAR_PLANE:
        pl.semaphore_signal(barrier, inc=1, device_id=plane(s), device_id_type=MESH)

    fetch = [
        pltpu.make_async_copy(points_ref, cols.at[0, pl.ds(0, B)], in_s.at[0]),
        pltpu.make_async_copy(panel_ref, panel, in_s.at[1]),
    ]
    for cp in fetch:
        cp.start()

    def fill(s, _):
        rows[s, W + AUG:, :] = jnp.zeros((W - AUG, B), jnp.bfloat16)
        return 0
    lax.fori_loop(0, 16, fill, 0)
    acc[...] = jnp.zeros_like(acc)
    for cp in fetch:
        cp.wait()

    pts = cols[0, :B, :]
    ptst = pts.astype(jnp.float32).T
    hi, mid, lo = three_terms(-0.5 * jnp.sum(ptst * ptst, axis=0, keepdims=True))
    row = lax.broadcasted_iota(jnp.int32, (AUG, B), 0)
    aug = jnp.where(row == 0, hi, jnp.where(row == 1, mid, jnp.where(row == 2, lo, 0.0)))
    aug = jnp.where((row >= 3) & (row < 6), 1.0, aug)
    rows[0, :W, :] = ptst.astype(jnp.bfloat16)
    rows[0, W:W + AUG, :] = aug.astype(jnp.bfloat16)
    cols[0, B:B + KC, :] = panel[:, :W]
    cols[0, B + KC:, :] = panel[:, W:]

    coef = LOG2E / (spread_ref[0] * spread_ref[0])

    def augment(s):
        xf = cols[s, :B, :].astype(jnp.float32)
        jh, jm, jl = three_terms(-0.5 * jnp.sum(xf * xf, axis=1, keepdims=True))
        lane = lax.broadcasted_iota(jnp.int32, (B, W), 1)
        ja = jnp.where(lane == 3, jh, jnp.where(lane == 4, jm, jnp.where(lane == 5, jl, 0.0)))
        colaug[s] = jnp.where(lane < 3, 1.0, ja).astype(jnp.bfloat16)

    augment(0)

    pl.semaphore_wait(barrier, len(NEAR_LINE) + len(NEAR_PLANE))

    def row_copy(s):
        t = plane_back(s)
        return pltpu.make_async_remote_copy(
            src_ref=rows.at[0, pl.ds(0, W + AUG)], dst_ref=rows.at[t, pl.ds(0, W + AUG)],
            send_sem=row_s.at[s], recv_sem=row_r.at[t], device_id=plane(s), device_id_type=MESH)

    def half_copy(src, to, dst, part, ss, rs):
        return pltpu.make_async_remote_copy(
            src_ref=rows.at[src, part], dst_ref=rows.at[dst, part],
            send_sem=ss.at[dst], recv_sem=rs.at[dst], device_id=plane(to), device_id_type=MESH)

    row_pass = {}
    for e in (1, 3, 2):
        for d in (1, 3, 2):
            src, to = PLANE.index((0, d)), PLANE.index((e, 0))
            row_pass.setdefault(src, []).append(
                half_copy(src, to, PLANE.index(((4 - e) % 4, d)), pl.ds(0, HALF), rowa_s, rowa_r))
            src, to = PLANE.index((d, 0)), PLANE.index((0, e))
            row_pass.setdefault(src, []).append(
                half_copy(src, to, PLANE.index((d, (4 - e) % 4)), pl.ds(HALF, W + AUG - HALF), rowb_s, rowb_r))

    def row_in(s):
        row_copy(plane_back(s)).wait_recv()
        for cp in row_pass[s]:
            cp.start()

    def halves_in(s):
        half_copy(0, 1, s, pl.ds(0, HALF), rowa_s, rowa_r).wait_recv()
        half_copy(0, 1, s, pl.ds(HALF, W + AUG - HALF), rowb_s, rowb_r).wait_recv()

    def col_copy(src, dst, sem, where, part=pl.ds(0, MSG), arrival=None):
        return pltpu.make_async_remote_copy(
            src_ref=cols.at[src, part], dst_ref=cols.at[dst, part],
            send_sem=sem, recv_sem=col_r.at[dst if arrival is None else arrival], device_id=where, device_id_type=MESH)

    def wait_col(s):
        col_copy(0, s, sib_s.at[0], line(1)).wait_recv()

    at = LINE.index
    half = MSG // 2
    col_pass = {
        0: [
            col_copy(0, at((1, 0)), fwd_s.at[0], line(at((7, 0)))),
            col_copy(0, at((7, 0)), fwd_s.at[1], line(at((1, 0)))),
            col_copy(0, at((0, 1)), sib_s.at[0], line(1)),
            col_copy(0, at((2, 0)), fwd_s.at[2], line(at((6, 0)))),
            col_copy(0, at((6, 0)), fwd_s.at[3], line(at((2, 0)))),
        ],
        at((1, 0)): [], at((7, 0)): [],
        at((2, 0)): [
            col_copy(at((2, 0)), at((3, 0)), fwd_s.at[4], line(at((7, 0)))),
            col_copy(at((2, 0)), at((4, 0)), fwd_s.at[6], line(at((6, 0))), pl.ds(0, half)),
        ],
        at((6, 0)): [
            col_copy(at((6, 0)), at((5, 0)), fwd_s.at[5], line(at((1, 0)))),
            col_copy(at((6, 0)), at((4, 0)), fwd_s.at[7], line(at((2, 0))), pl.ds(half, half), 16),
        ],
        at((3, 0)): [], at((5, 0)): [], at((4, 0)): [],
    }
    for dz in range(1, 8):
        s = at((dz, 0))
        col_pass[s].append(col_copy(s, at((dz, 1)), sib_s.at[dz], line(1)))
    row_sends = [row_copy(s) for s in (1, 2, 3, 4, 5, 6)]

    def col_in(s):
        if LINE[s] == (4, 0):
            col_pass[at((2, 0))][1].wait_recv()
            col_pass[at((6, 0))][1].wait_recv()
        else:
            wait_col(s)
        for cp in col_pass[s]:
            cp.start()

    for cp in col_pass[0][:3] + row_sends[:4] + col_pass[0][3:] + row_sends[4:]:
        cp.start()

    col_in(2)
    col_in(3)
    for s in (1, 2, 3, 4):
        row_in(s)
    wait_col(1)
    for s in (1, 2, 3):
        augment(s)

    ones = jnp.where(lax.broadcasted_iota(jnp.int32, (KR - KC, 16 * B), 0) < 2, 1.0, 0.0).astype(jnp.bfloat16)

    upper = lax.broadcasted_iota(jnp.int32, (8, L), 0) == 0

    def chunk(c0, nc, r0, nr, own=False):
        part = cols[pl.ds(c0, nc)]
        lhs = jnp.concatenate(
            [part[:, :B].reshape(nc * B, W), colaug[pl.ds(c0, nc)].reshape(nc * B, W)], axis=1)
        pt = jnp.concatenate(
            [part[k, B + h * KC:B + (h + 1) * KC] for k in range(nc) for h in range(2)], axis=1)
        pt = jnp.concatenate([pt, ones[:, :nc * B]], axis=0)
        rhs = jnp.concatenate([rows[r0 + k] for k in range(nr)], axis=1)
        g = jnp.dot(lhs, rhs, preferred_element_type=jnp.float32)
        a = jnp.exp2(g * coef)
        if own:
            eye = lax.broadcasted_iota(jnp.int32, (B, B), 0) == lax.broadcasted_iota(jnp.int32, (B, B), 1)
            first = jnp.where(eye, 0.0, a[:B])
            a = jnp.concatenate([first, a[B:]], axis=0)
        o = jnp.dot(pt, a.astype(jnp.bfloat16), preferred_element_type=jnp.float32)
        for k in range(nr):
            left, right = o[:, k * B:k * B + L], o[:, k * B + L:(k + 1) * B]
            acc[r0 + k, :KC] += left[:KC]
            acc[r0 + k, KC:2 * KC] += right[:KC]
            acc[r0 + k, 2 * KC:] += jnp.where(upper, left[KC:KC + 8], right[KC:KC + 8])

    chunk(0, 4, 1, 4)
    row_in(5)
    row_in(6)
    chunk(0, 4, 5, 2)
    wait_col(4)
    wait_col(5)
    augment(4)
    augment(5)
    chunk(4, 2, 1, 6)
    col_in(6)
    col_in(7)
    augment(6)
    augment(7)
    chunk(6, 2, 1, 6)
    def reduce_copy(s):
        t = plane_back(s)
        return pltpu.make_async_remote_copy(
            src_ref=acc.at[s], dst_ref=recvp.at[t],
            send_sem=red_s.at[s], recv_sem=red_r.at[t], device_id=plane(s), device_id_type=MESH)

    red = {s: reduce_copy(s) for s in range(1, 16)}

    def send_sums(slots):
        for s in slots:
            red[s].start()

    for s in range(8, 12):
        halves_in(s)
    chunk(0, 4, 8, 4)
    chunk(4, 4, 8, 4)
    col_in(10)
    col_in(11)
    for s in range(12, 16):
        halves_in(s)
    wait_col(8)
    wait_col(9)
    for s in range(8, 12):
        augment(s)
    chunk(0, 4, 12, 4)
    col_in(14)
    chunk(4, 4, 12, 4)
    wait_col(12)
    wait_col(13)
    for s in range(12, 15):
        augment(s)
    chunk(8, 4, 12, 4)
    wait_col(15)
    augment(15)
    chunk(12, 4, 12, 4)
    send_sums(range(12, 16))
    chunk(8, 8, 8, 4)
    send_sums(range(8, 12))
    halves_in(7)
    chunk(0, 8, 7, 1)
    chunk(8, 8, 4, 4)
    send_sums(range(4, 8))
    chunk(8, 8, 1, 3)
    send_sums(range(1, 4))
    chunk(0, 16, 0, 1, own=True)
    for cp in row_sends + sum(row_pass.values(), []) + sum(col_pass.values(), []):
        cp.wait_send()
    sums = acc[0]
    for s in range(15, 0, -1):
        red[plane_back(s)].wait_recv()
        sums = sums + recvp[s]
    walked = [sums[h * KC:(h + 1) * KC] / sums[2 * KC + h:2 * KC + h + 1] for h in range(2)]

    part = jnp.sum(walked[0] * walked[0] + walked[1] * walked[1], axis=1, keepdims=True)
    diag = lax.broadcasted_iota(jnp.int32, (KC, 128), 0) == lax.broadcasted_iota(jnp.int32, (KC, 128), 1)
    flat = jnp.sum(jnp.where(diag, part, 0.0), axis=0, keepdims=True)

    def stage(k, flat, where, back, ss, rs, before):
        st_send[k] = jnp.broadcast_to(flat, (8, 128))
        cps = []
        for s in range(15, 0, -1):
            cp = pltpu.make_async_remote_copy(
                src_ref=st_send.at[k], dst_ref=st_recv.at[k, back(s)],
                send_sem=ss.at[s], recv_sem=rs.at[back(s)],
                device_id=where(s), device_id_type=MESH)
            cp.start()
            cps.append(cp)
        for cp in before:
            cp.wait_send()
        for cp in cps:
            cp.wait_recv()
        for s in range(1, 16):
            flat = flat + st_recv[k, s, 0:1, :]
        return flat, cps

    flat, c1 = stage(0, flat, plane, plane_back, a_s, a_r, list(red.values()))
    flat, c2 = stage(1, flat, line, line_back, b_s, b_r, c1)
    mean = jnp.sum(jnp.where(diag, jnp.broadcast_to(flat, (KC, 128)), 0.0), axis=1, keepdims=True) / total
    scale = jnp.sqrt(mean + 1e-6)
    for h in range(2):
        out_ref[:, h * L:(h + 1) * L] = walked[h] / scale

    for cp in c2:
        cp.wait_send()


def per_device(total, points, spread, panel):
    dma = pltpu.SemaphoreType.DMA((24,))
    return pl.pallas_call(
        functools.partial(kernel, total),
        out_shape=jax.ShapeDtypeStruct((KC, B), jnp.float32),
        in_specs=[pl.BlockSpec(memory_space=pltpu.SMEM)] + [pl.BlockSpec(memory_space=pltpu.HBM)] * 2,
        out_specs=pl.BlockSpec(memory_space=pltpu.VMEM),
        scratch_shapes=[
            pltpu.VMEM((16, 2 * W, B), jnp.bfloat16),
            pltpu.VMEM((16, MSG, W), jnp.bfloat16),
            pltpu.VMEM((KC, B), jnp.bfloat16),
            pltpu.VMEM((16, B, W), jnp.bfloat16),
            pltpu.VMEM((16, KS, L), jnp.float32),
            pltpu.VMEM((16, KS, L), jnp.float32),
            pltpu.VMEM((2, 8, 128), jnp.float32),
            pltpu.VMEM((2, 16, 8, 128), jnp.float32),
        ] + [dma] * 17,
        compiler_params=pltpu.CompilerParams(
            collective_id=0, has_side_effects=True, vmem_limit_bytes=48 << 20),
        cost_estimate=pl.CostEstimate(flops=2 * 4096 * 4096 * 160, bytes_accessed=1 << 20, transcendentals=4096 * 4096),
        name="walk",
    )(spread, pltpu.with_memory_space_constraint(points, pltpu.HBM), pltpu.with_memory_space_constraint(panel.T, pltpu.HBM))


def solution(mesh):
    P = jax.sharding.PartitionSpec
    total = float(B * mesh.size)
    return jax.shard_map(
        functools.partial(per_device, total),
        mesh=mesh,
        in_specs=(P(("rowblk", "colblk"), None), P(), P(("rowblk", "colblk"), None)),
        out_specs=P(None, ("rowblk", "colblk")),
        check_vma=False,
    )
```
